32 devices in a mesh: table: 16 (over z, y, x), dp: 2 (over core).
Axes of the slice: x: 2, y: 2, z: 4, core: 2. Of those that a mesh axis runs over, the one named last changes fastest.
Arguments:
- emb_table: float32 [32768, 128], P('table'), may hold values from -4 to 4
- versions: int32 [32768], P('table'), may hold values from 0 to 999
- conf_local: int32 [4096], P('table'), may hold values from 0 to 2047, as said below
- conf_version: int32 [4096], P('table'), may hold values from 0 to 999
- conf_values: float32 [4096, 128], P('table'), may hold values from -4 to 4
- owners: int32 [4096, 26, 1], P(('table', 'dp')), may hold values from 0 to 15; in each aligned block of 3328 rows (0 to 3327, 3328 to 6655, ..., all dimensions but the last counted through in order) at most 312 rows name the same one
- row_local: int32 [4096, 26, 2], P(('table', 'dp')), may hold values from 0 to 2047
- lengths: int32 [4096, 26], P(('table', 'dp')), may hold values from 1 to 2
- dense_out: bfloat16 [4096, 128], P(('table', 'dp')), may hold values from -6 to 6
- labels: int32 [4096], P(('table', 'dp')), may hold values 0 or 1
- cross_down: bfloat16 [1, 3456, 512], P(None, None, 'dp'), may hold values from -0.109375 to 0.109375
- cross_up: bfloat16 [1, 512, 3456], P(None, 'dp'), may hold values from -0.25 to 0.25
- cross_bias: float32 [1, 3456], replicated, may hold values from -3 to 3
- head_weight: float32 [3456], replicated, may hold values from -0.109375 to 0.109375
Outputs:
- logits: float32 [4096], P(('table', 'dp'))
- emb_grad: float32 [32768, 128], P(('table', 'dp'))
The draws below stay inside these ranges and needn't reach their ends.
Inputs may be any that keep to these rules, and one draw needn't show every extreme that they name: `owners`: in each aligned block of the 3328 bags of one device (samples in order, bags within a sample in order), at most 312 bags name one holder; in some block one holder is named by exactly 312 bags. `conf_local`: within each holder's 256 entries the local row numbers are distinct.
All inputs are finite; a program needn't handle non-finite values. No bound on the sum of `labels` on one device may be relied on, other than what follows from the above.
Results may differ from the reference program's by a relative error of at most 0.0035.
Values may be sent and summed in bfloat16 or wider, within the bound.
No kernel may reach another device: no remote copies, remote signals or barrier semaphores. Data moves between devices by JAX's collectives and lax.ppermute only.
A program may use at most 64 MiB of HBM per device.

```python
import math
import jax
import jax.numpy as jnp
import numpy as np
from jax import lax

E = 128
F = 26
RANK = 512
LAYERS = 1
L = 2
B_DEV = 128
ROWS_DEV = 2048
CONF = 256
XW = 3456
CAP = 312
B = 4096
ROWS = 32768
NCONF = 4096
N_TABLE = 16


def draw_conf_local(key, part):
    holders = NCONF // CONF
    keys = jax.random.split(jax.random.fold_in(key, 11), holders)
    picks = jax.vmap(lambda single: jax.random.permutation(single, ROWS_DEV)[:CONF])(keys)
    parity = jnp.arange(holders, dtype=jnp.int32) % 2
    wanted = jnp.where(parity == 0, ROWS_DEV - 1, 0).astype(jnp.int32)
    offset = (wanted - picks[:, 0].astype(jnp.int32)) % ROWS_DEV
    shifted = (picks.astype(jnp.int32) + offset[:, None]) % ROWS_DEV
    return shifted.reshape(NCONF).astype(jnp.int32)


def place_ends(array, rng, low, high):
    longest = array.shape.index(max(array.shape))
    spots = []
    for shift in (0, 1):
        where = [jax.random.randint(jax.random.fold_in(rng, axis), (), 0, length) for axis, length in enumerate(array.shape)]
        where[longest] = (where[longest] + shift) % array.shape[longest]
        spots.append(tuple(where))
    return array.at[spots[0]].set(low).at[spots[1]].set(high)


def block_scale(own_key, shape, cuts, least, largest):
    gain = 1.0
    for axis_at, blocks in cuts:
        draws = jax.random.uniform(jax.random.fold_in(jax.random.fold_in(own_key, 6), axis_at), (blocks,), jnp.float32, least / len(cuts), largest / len(cuts))
        gain = gain * jnp.repeat(jnp.exp(draws), shape[axis_at] // blocks).reshape((-1,) + (1,) * (len(shape) - 1 - axis_at))
    return gain


def cumulative_ranks(count, skew):
    portions = [(1 << 20) // math.isqrt(grade ** skew) + 1 for grade in range(1, count + 1)]
    deviation = 1 + sum(portions) // (1 << 30)
    return np.cumsum(np.array([max(1, weight // deviation) for weight in portions]))


def ranked_ids(own_key, dims, number_of, skew):
    grid = cumulative_ranks(number_of, skew)
    pick = jax.random.randint(jax.random.fold_in(own_key, 1), dims, 0, int(grid[number_of - 1]))
    standing = jnp.searchsorted(jnp.asarray(grid, jnp.int32), pick, side="right")
    return jax.random.permutation(jax.random.fold_in(own_key, 2), number_of)[standing].astype(jnp.int32)


def assign_block(stream_key, own, number, rows, number_of, top, bound, skew):
    order = jax.random.permutation(stream_key, number_of)
    heavy_load, common = portions_of(number_of, rows * top, bound, skew, True), portions_of(number_of, rows * top, bound, skew, False)
    places = jnp.arange(number_of)

    def named(sizes, turn):
        used = int((sizes > 0).sum())
        fixed = max(1, used // 4)
        moved = fixed + (places - fixed + turn * (used - fixed)) % max(1, number_of - fixed)
        return jnp.zeros((number_of,), jnp.int32).at[order[jnp.where(places < fixed, places, moved)]].set(jnp.asarray(sizes, jnp.int32))

    sizes = jnp.where(number % 4 == 0, named(heavy_load, number // 4), named(common, number - number // 4 - 1))
    mixed = jax.random.permutation(jax.random.fold_in(own, 3), number_of)
    giver, taker = mixed[0:number_of // 2 * 2:2], mixed[1:number_of // 2 * 2:2]
    room = jnp.minimum(sizes[giver] - 1, bound - sizes[taker]) // 2
    room = jnp.where((giver == order[0]) | (taker == order[0]) | (sizes[taker] == 0), 0, jnp.maximum(room, 0))
    moved = jax.random.randint(jax.random.fold_in(own, 4), (number_of // 2,), 0, 1 << 20) % (room + 1)
    sizes = sizes.at[giver].add(-moved).at[taker].add(moved)
    members = jnp.searchsorted(jnp.cumsum(sizes), jnp.arange(rows * top), side="right").astype(jnp.int32)
    listing = members.reshape(top, rows).T
    listing = listing[jax.random.permutation(jax.random.fold_in(own, 1), rows)]
    turn = jax.random.randint(jax.random.fold_in(own, 2), (rows, 1), 0, top)
    return jnp.take_along_axis(listing, (jnp.arange(top)[None, :] + turn) % top, axis=1)


def portions_of(number_of, total, reach, slope, full):
    loads = [(1 << 20) // math.isqrt(rank ** slope) + 1 for rank in range(1, number_of + 1)]
    largest = reach if full else min(reach, max(-(-total // number_of), total * loads[0] // sum(loads)))
    least = 1 if total - largest >= number_of - 1 else 0
    holding, spare = [largest] + [least] * (number_of - 1), total - largest - least * (number_of - 1)
    while spare > 0:
        movable = [i for i in range(1, number_of) if holding[i] < largest] or [i for i in range(1, number_of) if holding[i] < reach]
        mass, left = sum([loads[i] for i in movable]), spare
        for i in movable:
            extra = min(reach - holding[i], max(1, left * loads[i] // mass), spare)
            holding[i] = holding[i] + extra
            spare = spare - extra
    return np.array(holding)


def scatter_about(own_key, dims, scale, bound, cuts=(), kind=jnp.bfloat16):
    drawn = jax.random.normal(own_key, dims, jnp.float32) * scale
    if len(cuts) > 0:
        drawn = block_scale(own_key, dims, cuts, -0.22, 0.18) * drawn
    return jnp.clip(drawn, min=-bound, max=bound).astype(kind)


def setup_inputs(seed: int = 0) -> dict:
    seeds = jax.random.split(jax.random.key(seed), 15)
    emb_table = scatter_about(seeds[0], (ROWS, E), 0.5, 4.0, ((0, 16),), jnp.float32)
    versions = place_ends(jax.random.randint(seeds[1], (ROWS,), 0, 1000), jax.random.fold_in(seeds[1], 1), 0, 999).astype(jnp.int32)
    conf_local = draw_conf_local(jax.random.fold_in(seeds[14], 71), 0)
    conf_version = place_ends(jax.random.randint(seeds[3], (NCONF,), 0, 1000), jax.random.fold_in(seeds[3], 1), 0, 999).astype(jnp.int32)
    conf_values = scatter_about(seeds[4], (NCONF, E), 0.5, 4.0, ((0, 16),), jnp.float32)
    owners_keys = jax.random.split(jax.random.fold_in(seeds[5], 1), B * F // (B_DEV * F))
    owners_turns = jax.random.permutation(jax.random.fold_in(seeds[5], 3), B * F // (B_DEV * F))
    owners = jax.vmap(lambda own, number: assign_block(jax.random.fold_in(seeds[5], 2), own, number, B_DEV * F, N_TABLE, 1, CAP, 2))(owners_keys, owners_turns).reshape((B, F, 1))
    row_local = place_ends(ranked_ids(seeds[6], (B, F, L), ROWS_DEV, 2), jax.random.fold_in(seeds[6], 3), 0, ROWS_DEV - 1).astype(jnp.int32)
    lengths = place_ends(jax.random.randint(seeds[7], (B, F), 1, L + 1), jax.random.fold_in(seeds[7], 1), 1, L).astype(jnp.int32)
    dense_out = scatter_about(seeds[8], (B, E), 1.0, 6.0, ((0, 32),))
    labels = place_ends((jax.random.randint(seeds[9], (B,), 0, 4) < 1).astype(jnp.int32), jax.random.fold_in(seeds[9], 1), 0, 1)
    cross_down = scatter_about(seeds[10], (LAYERS, XW, RANK), XW ** -0.5, 0.109375, ((2, 2),))
    cross_up = scatter_about(seeds[11], (LAYERS, RANK, XW), RANK ** -0.5, 0.25, ((1, 2),))
    cross_bias = scatter_about(seeds[12], (LAYERS, XW), 0.5, 3.0, (), jnp.float32)
    head_weight = scatter_about(seeds[13], (XW,), XW ** -0.5, 0.109375, (), jnp.float32)
    return dict(emb_table=emb_table, versions=versions, conf_local=conf_local, conf_version=conf_version, conf_values=conf_values, owners=owners, row_local=row_local, lengths=lengths, dense_out=dense_out, labels=labels, cross_down=cross_down, cross_up=cross_up, cross_bias=cross_bias, head_weight=head_weight)


loss_scale = 64.0


def dense_step(inputs, labels, cross_down, cross_up, cross_bias, head_weight):
    base_float = inputs.astype(jnp.float32)
    state = base_float
    state_in = inputs
    factors = []
    layer_count = cross_down.shape[0]
    for cross_index in range(layer_count):
        crossed = jnp.dot(state_in, cross_down[cross_index], preferred_element_type=jnp.float32).astype(jnp.bfloat16)
        factor = jnp.dot(crossed, cross_up[cross_index], preferred_element_type=jnp.float32) + cross_bias[cross_index]
        factors.append(factor)
        state = base_float * factor + state
        state_in = state.astype(jnp.bfloat16)
    logits = jnp.sum(state * head_weight, axis=1)
    signal = loss_scale * (jax.nn.sigmoid(logits) - labels.astype(jnp.float32))
    grad_state = signal[:, None] * head_weight[None, :]
    grad_base = jnp.zeros_like(grad_state)
    for cross_index in range(layer_count - 1, -1, -1):
        grad_base = grad_base + grad_state * factors[cross_index]
        grad_lift = (grad_state * base_float).astype(jnp.bfloat16)
        grad_cross = lax.dot_general(grad_lift, cross_up[cross_index], (((1,), (1,)), ((), ())), preferred_element_type=jnp.float32).astype(jnp.bfloat16)
        grad_state = grad_state + lax.dot_general(grad_cross, cross_down[cross_index], (((1,), (1,)), ((), ())), preferred_element_type=jnp.float32)
    return logits, grad_state + grad_base


def reference(emb_table, versions, conf_local, conf_version, conf_values, owners, row_local, lengths, dense_out, labels, cross_down, cross_up, cross_bias, head_weight):
    holder = (jnp.arange(NCONF) // CONF).astype(jnp.int32)
    target = holder * ROWS_DEV + conf_local.astype(jnp.int32)
    is_newer = conf_version > versions[target]
    updated = emb_table.at[target].set(jnp.where(is_newer[:, None], conf_values, emb_table[target]))
    row_ids = (owners * ROWS_DEV + row_local).astype(jnp.int32)
    live_mask = jnp.arange(L, dtype=jnp.int32)[None, None, :] < lengths[:, :, None]
    per_block = B // N_TABLE
    block_ids = row_ids.reshape(N_TABLE, per_block, F, L)
    block_live = live_mask.reshape(N_TABLE, per_block, F, L)
    block_dense = dense_out.reshape(N_TABLE, per_block, E)
    block_labels = labels.reshape(N_TABLE, per_block)

    def scan_step(accumulated, pieces):
        piece_ids, piece_live, piece_dense, piece_labels = pieces
        looked_up = jnp.where(piece_live[..., None], updated[piece_ids], 0.0)
        pooled = jnp.sum(looked_up, axis=2).reshape(per_block, F * E)
        inputs = jnp.concatenate([piece_dense.astype(jnp.float32), pooled], axis=1).astype(jnp.bfloat16)
        piece_logits, grad_input = dense_step(inputs, piece_labels, cross_down, cross_up, cross_bias, head_weight)
        bag_grad = grad_input[:, E:].reshape(per_block, F, 1, E)
        updates = jnp.where(piece_live[..., None], bag_grad, 0.0)
        accumulated = accumulated.at[piece_ids.reshape(-1)].add(updates.reshape(-1, E))
        return accumulated, piece_logits

    start_grad = jnp.zeros((ROWS, E), jnp.float32)
    emb_grad, logit_blocks = lax.scan(scan_step, start_grad, (block_ids, block_live, block_dense, block_labels))
    return logit_blocks.reshape(B), emb_grad
```

```python
import functools

import jax
import jax.numpy as jnp
from jax import lax
from jax.experimental import pallas as pl
from jax.experimental.pallas import tpu as pltpu
from jax.sharding import PartitionSpec as P

loss_scale = 64.0
LANES = 128
F32, BF16, I32 = jnp.float32, jnp.bfloat16, jnp.int32
VMEM = pl.BlockSpec(memory_space=pltpu.VMEM)
SMEM = pl.BlockSpec(memory_space=pltpu.SMEM)
params = pltpu.CompilerParams(vmem_limit_bytes=56 * 1024 * 1024)
NT = (((1,), (1,)), ((), ()))


def dot(a, b, dims=(((1,), (0,)), ((), ()))):
    return lax.dot_general(a, b, dims, preferred_element_type=F32)


def iota(shape, axis):
    return lax.broadcasted_iota(I32, shape, axis)


def round_up(value, step):
    return -(-value // step) * step


def route_kernel(peers, cap, owner_ref, rows_ref, len_ref, pos_ref, req_ref, own_s, a_s, b_s):
    feats, lanes = len_ref.shape
    padded = own_s.shape[0]
    chunks = -(-cap // LANES)
    per = req_ref.shape[0] // peers
    count = peers * per
    own_s[...] = jnp.full(own_s.shape, -1, I32)
    own_s[0:feats, :] = owner_ref[...]
    own = own_s[...]
    hits = [(own == o).astype(F32) for o in range(peers)]
    stacked = jnp.concatenate(hits, axis=0).astype(BF16)
    row, col = iota((lanes, 2 * lanes), 0), iota((lanes, 2 * lanes), 1)
    upper = jnp.where((row < col) | (col >= lanes), 1.0, 0.0).astype(BF16)
    sums = dot(stacked, upper)
    totals = jnp.concatenate(
        [sums[o * padded : (o + 1) * padded, lanes:] for o in range(peers)], axis=1
    ).astype(BF16)
    lower = jnp.where(iota((padded, padded), 1) < iota((padded, padded), 0), 1.0, 0.0).astype(BF16)
    base = dot(lower, totals)
    rank = jnp.zeros((padded, lanes), F32)
    for o in range(peers):
        before = sums[o * padded : (o + 1) * padded, :lanes] + base[:, o * lanes : (o + 1) * lanes]
        rank = rank + hits[o] * before
    rank = rank.astype(I32)
    pos_ref[...] = (own * cap + rank)[0:feats, :]
    first = own * per + lax.shift_right_logical(rank, 7)
    second = first + chunks
    low = rank & (LANES - 1)
    lengths = len_ref[...]
    slots = rows_ref.shape[0] // feats
    ids = [
        jnp.where(lengths > slot, rows_ref[pl.ds(slot, feats, slots), :] + 1, 0)
        for slot in range(slots)
    ]
    at = iota((count, lanes), 0)
    lane_at = iota((LANES, lanes), 0)
    for f in range(feats):
        held = jnp.where(at == first[f : f + 1, :], ids[0][f : f + 1, :], 0)
        held = jnp.where(at == second[f : f + 1, :], ids[1][f : f + 1, :], held)
        span = slice(f * lanes, (f + 1) * lanes)
        a_s[0:count, span] = lax.shift_right_logical(held, 7).astype(F32).astype(BF16)
        a_s[count : 2 * count, span] = (held & 127).astype(F32).astype(BF16)
        b_s[:, span] = jnp.where(lane_at == low[f : f + 1, :], 1.0, 0.0).astype(BF16)
    found = dot(a_s[...], b_s[...], NT)
    req_ref[...] = (found[0:count] * 128.0 + found[count:]).astype(I32)


def update_kernel(local_ref, new_ref, versions_ref, table_ref, values_ref, out_ref, rows_s):
    rows_s[...] = table_ref[...]

    def entry(i, carry):
        at = local_ref[i]

        @pl.when(new_ref[i] > versions_ref[at])
        def _():
            rows_s[pl.ds(at, 1), :] = values_ref[pl.ds(i, 1), :]

        return carry

    lax.fori_loop(0, values_ref.shape[0], entry, 0, unroll=8)
    table = rows_s[...]
    width = table.shape[1]
    high = table.astype(BF16)
    out_ref[:, 0:width] = high
    out_ref[:, width:] = (table - high.astype(F32)).astype(BF16)


def lookup_kernel(peers, cap, ids_ref, table_ref, out_ref):
    rows, double = table_ref.shape
    width = double // 2
    per = ids_ref.shape[0] // peers
    chunks = -(-cap // LANES)

    def source(s, carry):
        block = ids_ref[pl.ds(pl.multiple_of(s * per, 8), per), :].T
        for c in range(chunks):
            n = min(LANES, cap - c * LANES)
            at = iota((n, rows), 1) + 1
            counts = jnp.where(at == block[0:n, c : c + 1], 1.0, 0.0) + jnp.where(
                at == block[0:n, chunks + c : chunks + c + 1], 1.0, 0.0
            )
            both = dot(counts.astype(BF16), table_ref[...])
            start = pl.multiple_of(s * cap + c * LANES, 16)
            out_ref[pl.ds(start, n), :] = (both[:, 0:width] + both[:, width:]).astype(BF16)
        return carry

    lax.fori_loop(0, peers, source, 0)


def dense_kernel(pieces, *refs):
    pos_ref, ans_ref, dense_ref, labels_ref = refs[0:4]
    down = refs[4 : 4 + pieces]
    up = refs[4 + pieces : 4 + 2 * pieces]
    bias_ref, head_ref, logit_ref, send_ref, rows_s, x_s, factor_s, bags_s = refs[4 + 2 * pieces :]
    feats, samples = pos_ref.shape
    width = dense_ref.shape[1]
    slots = ans_ref.shape[0]
    rows_s[...] = ans_ref[...].astype(F32)

    def fetch(f, carry):
        start = f * samples
        for b in range(samples):
            bags_s[pl.ds(start + b, 1), :] = rows_s[pl.ds(pos_ref[f, b], 1), :]
        return carry

    lax.fori_loop(0, feats, fetch, 0)
    x_s[:, 0:width] = dense_ref[...]
    for f in range(feats):
        x_s[:, (f + 1) * width : (f + 2) * width] = bags_s[
            f * samples : (f + 1) * samples, :
        ].astype(BF16)
    rows_s[...] = jnp.zeros(rows_s.shape, F32)
    x = x_s[...]
    crossed = [dot(x, w[...]).astype(BF16) for w in down]
    total = jnp.zeros((samples, width), F32)
    blocks = feats + 1
    for k in range(blocks):
        span = slice(k * width, (k + 1) * width)
        factor = bias_ref[:, span]
        for c, w in zip(crossed, up):
            factor = factor + dot(c, w[:, span])
        factor_s[:, span] = factor
        base = x_s[:, span].astype(F32)
        total = total + (base * factor + base) * head_ref[:, span]
    logits = jnp.sum(total, axis=1, keepdims=True)
    logit_ref[...] = logits
    signal = loss_scale * (jax.nn.sigmoid(logits) - labels_ref[...].astype(F32))
    lifts = []
    for k in range(blocks):
        span = slice(k * width, (k + 1) * width)
        lifts.append(((signal * head_ref[:, span]) * x_s[:, span].astype(F32)).astype(BF16))
    lift = jnp.concatenate(lifts, axis=1)
    back = [dot(lift, w[...], NT).astype(BF16) for w in up]
    for f in range(feats):
        span = slice((f + 1) * width, (f + 2) * width)
        outer = signal * head_ref[:, span]
        grad = outer
        for c, w in zip(back, down):
            grad = grad + dot(c, w[span, :], NT)
        bags_s[f * samples : (f + 1) * samples, :] = grad + outer * factor_s[:, span]

    def place(f, carry):
        start = f * samples
        for b in range(samples):
            rows_s[pl.ds(pos_ref[f, b], 1), :] = bags_s[pl.ds(start + b, 1), :]
        return carry

    lax.fori_loop(0, feats, place, 0)
    send_ref[...] = rows_s[...].astype(BF16)


def scatter_kernel(base_ref, ids_ref, grad_ref, out_ref):
    rows = out_ref.shape[0]
    lines = ids_ref.shape[0] // 2
    step = 4 if lines % 4 == 0 else 1
    at = iota((rows, LANES), 0) + 1 + base_ref[0]
    out_ref[...] = jnp.zeros(out_ref.shape, F32)

    def part(k, carry):
        counts = []
        for j in range(step):
            line = k * step + j
            one = ids_ref[pl.ds(line, 1), :]
            two = ids_ref[pl.ds(lines + line, 1), :]
            counts.append(
                (jnp.where(at == one, 1.0, 0.0) + jnp.where(at == two, 1.0, 0.0)).astype(BF16)
            )
        start = pl.multiple_of(k * (step * LANES), step * LANES)
        out_ref[...] += dot(
            jnp.concatenate(counts, axis=1), grad_ref[pl.ds(start, step * LANES), :]
        )
        return carry

    lax.fori_loop(0, lines // step, part, 0)


def call(kernel, outs, ins, scratch=()):
    return pl.pallas_call(
        kernel,
        out_shape=outs,
        in_specs=ins,
        out_specs=jax.tree.map(lambda _: VMEM, outs),
        scratch_shapes=list(scratch),
        compiler_params=params,
    )


def shape(dims, dtype):
    return jax.ShapeDtypeStruct(dims, dtype)


def body(
    emb_table,
    versions,
    conf_local,
    conf_version,
    conf_values,
    owners,
    row_local,
    lengths,
    dense_out,
    labels,
    cross_down,
    cross_up,
    cross_bias,
    head_weight,
):
    peers, replicas = lax.axis_size("table"), lax.axis_size("dp")
    dp_at = lax.axis_index("dp")
    rows_dev, width = emb_table.shape
    samples, feats, slots = row_local.shape
    cap = round_up(3 * samples * feats // (2 * peers), 16)
    chunks = -(-cap // LANES)
    per = round_up(slots * chunks, 8)
    total = round_up(peers * cap, LANES)
    wide = cross_down.shape[1]
    rank_dev = cross_down.shape[2]

    def shift(x, by):
        if by == 0:
            return x
        return lax.ppermute(x, "dp", [(i, (i + by) % replicas) for i in range(replicas)])

    down = [shift(cross_down[0], by) for by in range(replicas)]
    up = [shift(cross_up[0], by) for by in range(replicas)]

    position, requests = call(
        functools.partial(route_kernel, peers, cap),
        (shape((feats, samples), I32), shape((peers * per, LANES), I32)),
        [VMEM] * 3,
        [
            pltpu.VMEM((round_up(feats, 8), samples), I32),
            pltpu.VMEM((2 * peers * per, feats * samples), BF16),
            pltpu.VMEM((LANES, feats * samples), BF16),
        ],
    )(
        owners.reshape(samples, feats).T,
        row_local.transpose(1, 2, 0).reshape(feats * slots, samples),
        lengths.T,
    )
    asked = lax.all_to_all(
        requests.reshape(peers, per, LANES), "table", split_axis=0, concat_axis=0, tiled=True
    )
    updated = call(
        update_kernel,
        shape((rows_dev, 2 * width), BF16),
        [SMEM] * 3 + [VMEM] * 2,
        [pltpu.VMEM((rows_dev, width), F32)],
    )(conf_local, conf_version, versions, emb_table, conf_values)
    found = call(
        functools.partial(lookup_kernel, peers, cap),
        shape((peers * cap, width), BF16),
        [VMEM] * 2,
    )(asked.reshape(peers * per, LANES), updated)
    answer = lax.all_to_all(
        found.reshape(peers, cap, width), "table", split_axis=0, concat_axis=0, tiled=True
    )
    logits, send = call(
        functools.partial(dense_kernel, replicas),
        (shape((samples, 1), F32), shape((peers * cap, width), BF16)),
        [SMEM] + [VMEM] * (5 + 2 * replicas),
        [
            pltpu.VMEM((peers * cap, width), F32),
            pltpu.VMEM((samples, wide), BF16),
            pltpu.VMEM((samples, wide), F32),
            pltpu.VMEM((samples * feats, width), F32),
        ],
    )(
        position,
        answer.reshape(peers * cap, width),
        dense_out,
        labels.reshape(samples, 1),
        *down,
        *up,
        cross_bias,
        head_weight.reshape(1, wide),
    )
    got = lax.all_to_all(
        send.reshape(peers, cap, width), "table", split_axis=0, concat_axis=0, tiled=True
    ).reshape(peers * cap, width)
    lines = jnp.concatenate(
        [
            asked[:, slot * chunks : (slot + 1) * chunks]
            .reshape(peers, chunks * LANES)[:, :cap]
            .reshape(total // LANES, LANES)
            for slot in range(slots)
        ]
    )
    own_rows = rows_dev // replicas
    grads = None
    for by in range(replicas - 1, -1, -1):
        target = lax.rem(dp_at + by, replicas)
        part = call(
            scatter_kernel, shape((own_rows, width), F32), [SMEM] + [VMEM] * 2
        )((target * own_rows).astype(I32).reshape(1), lines, got)
        part = shift(part, by)
        grads = part if grads is None else grads + part
    return (logits.reshape(samples), grads)


def solution(mesh):
    in_specs = (
        P("table", None),
        P("table"),
        P("table"),
        P("table"),
        P("table", None),
        P(("table", "dp"), None, None),
        P(("table", "dp"), None, None),
        P(("table", "dp"), None),
        P(("table", "dp"), None),
        P(("table", "dp")),
        P(None, None, "dp"),
        P(None, "dp", None),
        P(),
        P(),
    )
    out_specs = (P(("table", "dp")), P(("table", "dp"), None))
    return jax.shard_map(body, mesh=mesh, in_specs=in_specs, out_specs=out_specs, check_vma=False)
```

```python
import functools

import jax
import jax.numpy as jnp
from jax import lax
from jax.experimental import pallas as pl
from jax.experimental.pallas import tpu as pltpu
from jax.sharding import PartitionSpec as P

loss_scale = 64.0
LANES = 128
F32, BF16, I32, I16 = jnp.float32, jnp.bfloat16, jnp.int32, jnp.int16
VMEM = pl.BlockSpec(memory_space=pltpu.VMEM)
SMEM = pl.BlockSpec(memory_space=pltpu.SMEM)
ANY = pl.BlockSpec(memory_space=pl.ANY)
params = pltpu.CompilerParams(vmem_limit_bytes=36 * 1024 * 1024)
NT = (((1,), (1,)), ((), ()))


def dot(a, b, dims=(((1,), (0,)), ((), ()))):
    return lax.dot_general(a, b, dims, preferred_element_type=F32)


def iota(shape, axis):
    return lax.broadcasted_iota(I32, shape, axis)


def round_up(value, step):
    return -(-value // step) * step


def route_kernel(
    peers, cap, owner_ref, rows_ref, len_ref, pos_ref, req_ref, own_s, one_s, two_s, a_s, b_s
):
    feats, lanes = len_ref.shape
    padded = own_s.shape[0]
    chunks = -(-cap // LANES)
    half = peers // 2
    per = req_ref.shape[0] // peers
    count = peers * per
    own_s[...] = jnp.full(own_s.shape, -1, I32)
    for f in range(feats):
        own_s[f : f + 1, :] = owner_ref[f]
        one_s[f : f + 1, :] = rows_ref[f, 0:1, :]
        two_s[f : f + 1, :] = rows_ref[f, 1:2, :]
    own = own_s[...]
    hits = [(own == o).astype(F32) for o in range(peers)]
    stacked = jnp.concatenate(hits, axis=0).astype(BF16)
    row, col = iota((lanes, 2 * lanes), 0), iota((lanes, 2 * lanes), 1)
    upper = jnp.where((row < col) | (col >= lanes), 1.0, 0.0).astype(BF16)
    sums = dot(stacked, upper)
    totals = jnp.concatenate(
        [sums[o * padded : (o + 1) * padded, lanes:] for o in range(peers)], axis=1
    ).astype(BF16)
    lower = jnp.where(iota((padded, padded), 1) < iota((padded, padded), 0), 1.0, 0.0).astype(BF16)
    base = dot(lower, totals)
    rank = jnp.zeros((padded, lanes), F32)
    for o in range(peers):
        before = sums[o * padded : (o + 1) * padded, :lanes] + base[:, o * lanes : (o + 1) * lanes]
        rank = rank + hits[o] * before
    rank = rank.astype(I32)
    far = own >= half
    column = jnp.where(far, own - half, own)
    side = (lax.axis_index("table") >= half).astype(I32)
    mirrored = jnp.where(far, 1 - side, side)
    place = jnp.where(own < 0, -8, column * 2 + mirrored)
    pos_ref[...] = (place * cap + rank)[0:feats, :]
    first = place * per + lax.shift_right_logical(rank, 7)
    second = first + chunks
    low = rank & (LANES - 1)
    lengths = len_ref[...]
    one = jnp.where(lengths > 0, one_s[0:feats, :] + 1, 0)
    two = jnp.where(lengths > 1, two_s[0:feats, :] + 1, 0)
    at = iota((count, lanes), 0)
    lane_at = iota((LANES, lanes), 0)
    for f in range(feats):
        held = jnp.where(at == first[f : f + 1, :], one[f : f + 1, :], 0)
        held = jnp.where(at == second[f : f + 1, :], two[f : f + 1, :], held)
        span = slice(f * lanes, (f + 1) * lanes)
        a_s[0:count, span] = lax.shift_right_logical(held, 7).astype(F32).astype(BF16)
        a_s[count : 2 * count, span] = (held & 127).astype(F32).astype(BF16)
        b_s[:, span] = jnp.where(lane_at == low[f : f + 1, :], 1.0, 0.0).astype(BF16)
    found = dot(a_s[...], b_s[...], NT)
    req_ref[...] = (found[0:count] * 128.0 + found[count:]).astype(I32)


def update_kernel(
    after_ref, local_ref, new_ref, versions_ref, table_ref, values_ref, table_out_ref, part_ref, rows_s
):
    del after_ref
    held_rows, width = table_ref.shape
    rows_s[0:held_rows, :] = table_ref[...]

    def entry(i, carry):
        at = local_ref[i]
        to = jnp.where(new_ref[i] > versions_ref[at], at, held_rows)
        rows_s[pl.ds(to, 1), :] = values_ref[pl.ds(i, 1), :]
        return carry

    lax.fori_loop(0, values_ref.shape[0], entry, 0, unroll=8)
    table = rows_s[0:held_rows, :]
    high = table.astype(BF16)
    table_out_ref[:, 0:width] = high
    table_out_ref[:, width:] = (table - high.astype(F32)).astype(BF16)
    own_rows = part_ref.shape[0]
    start = pl.multiple_of(lax.axis_index("dp") * own_rows, own_rows)
    part_ref[...] = rows_s[pl.ds(start, own_rows), :].astype(BF16)


def lookup_kernel(kind, peers, cap, ids_ref, *refs):
    out_ref, count_s, found_s, sems = refs[-4:]
    tables = refs[:-4] if kind == 0 else refs[1:-4]
    width = out_ref.shape[1]
    per = ids_ref.shape[0] // (2 * peers)
    chunks = -(-cap // LANES)
    group = count_s.shape[1] // cap
    one, zero = jnp.ones((), BF16), jnp.zeros((), BF16)
    pieces = len(tables)
    at_dp = lax.axis_index("dp")
    bases = [lax.rem(at_dp + pieces - p, pieces) * tables[p].shape[0] for p in range(pieces)]

    def count(i):
        for g in range(group):
            start = ((i * group + g) * 2 + kind) * per
            block = ids_ref[start : start + per, :].T
            for c in range(chunks):
                n = min(LANES, cap - c * LANES)
                at = g * cap + c * LANES
                a = jnp.broadcast_to(block[0:n, c : c + 1], (n, LANES))
                b = jnp.broadcast_to(block[0:n, chunks + c : chunks + c + 1], (n, LANES))
                column = 0
                for p, table in enumerate(tables):
                    a16 = (a - bases[p]).astype(I16)
                    b16 = (b - bases[p]).astype(I16)
                    for k in range(0, table.shape[0], LANES):
                        size = min(LANES, table.shape[0] - k)
                        row = (iota((n, size), 1) + (1 + k)).astype(I16)
                        count_s[i % 2, at : at + n, column : column + size] = jnp.where(
                            a16[:, :size] == row, one, zero
                        ) + jnp.where(b16[:, :size] == row, one, zero)
                        column += size

    def multiply(i):
        total = None
        column = 0
        for table in tables:
            rows, span = table.shape
            both = dot(count_s[i % 2, :, column : column + rows], table[...])
            if span > width:
                both = both[:, 0:width] + both[:, width:]
            total = both if total is None else total + both
            column += rows
        found_s[i * group * cap : (i + 1) * group * cap, :] = total.astype(BF16)

    def move(source):
        return pltpu.make_async_copy(
            found_s.at[source * cap : (source + 1) * cap, :],
            out_ref.at[(2 * source + kind) * cap : (2 * source + kind + 1) * cap, :],
            sems.at[source],
        )

    steps = peers // group
    count(0)
    for i in range(steps):
        if i + 1 < steps:
            count(i + 1)
        multiply(i)
        for source in range(i * group, (i + 1) * group):
            move(source).start()
    for source in range(peers):
        move(source).wait()


def dense_kernel(pieces, *refs):
    pos_ref, answer_ref, dense_ref, labels_ref = refs[0:4]
    (
        bias_ref, head_ref, logit_ref, send_ref, rows_s, x_s, factor_s, bags_s, down_s, up_s, sems,
    ) = refs[4 + 2 * pieces :]
    loads = []
    for p in range(pieces):
        loads.append(pltpu.make_async_copy(refs[4 + p], down_s.at[p], sems.at[p]))
    for p in range(pieces):
        loads.append(pltpu.make_async_copy(refs[4 + pieces + p], up_s.at[p], sems.at[pieces + p]))
    for load in loads:
        load.start()
    down = [down_s.at[p] for p in range(pieces)]
    up = [up_s.at[p] for p in range(pieces)]
    feats, samples = pos_ref.shape
    width = dense_ref.shape[1]
    rows_s[...] = answer_ref[...].astype(F32)

    def fetch(f, carry):
        start = f * samples
        for b in range(samples):
            bags_s[pl.ds(start + b, 1), :] = rows_s[pl.ds(pos_ref[f, b], 1), :]
        return carry

    lax.fori_loop(0, feats, fetch, 0)
    x_s[:, 0:width] = dense_ref[...]
    for f in range(feats):
        x_s[:, (f + 1) * width : (f + 2) * width] = bags_s[
            f * samples : (f + 1) * samples, :
        ].astype(BF16)
    rows_s[...] = jnp.zeros(rows_s.shape, F32)
    for load in loads:
        load.wait()
    x = x_s[...]
    crossed = [dot(x, w[...]).astype(BF16) for w in down]
    total = jnp.zeros((samples, width), F32)
    blocks = feats + 1
    for k in range(blocks):
        span = slice(k * width, (k + 1) * width)
        factor = bias_ref[:, span]
        for c, w in zip(crossed, up):
            factor = factor + dot(c, w[:, span])
        factor_s[:, span] = factor
        base = x_s[:, span].astype(F32)
        total = total + (base * factor + base) * head_ref[:, span]
    logits = jnp.sum(total, axis=1, keepdims=True)
    logit_ref[...] = jnp.broadcast_to(logits, (samples, samples)).T[0:1, :]
    labels = jnp.broadcast_to(labels_ref[...].astype(F32), (samples, samples)).T[:, 0:1]
    signal = loss_scale * (jax.nn.sigmoid(logits) - labels)
    lifts = []
    for k in range(blocks):
        span = slice(k * width, (k + 1) * width)
        lifts.append(((signal * head_ref[:, span]) * x_s[:, span].astype(F32)).astype(BF16))
    lift = jnp.concatenate(lifts, axis=1)
    back = [dot(lift, w[...], NT).astype(BF16) for w in up]
    for f in range(feats):
        span = slice((f + 1) * width, (f + 2) * width)
        outer = signal * head_ref[:, span]
        grad = outer
        for c, w in zip(back, down):
            grad = grad + dot(c, w[span, :], NT)
        bags_s[f * samples : (f + 1) * samples, :] = grad + outer * factor_s[:, span]

    def place(f, carry):
        start = f * samples
        for b in range(samples):
            rows_s[pl.ds(pos_ref[f, b], 1), :] = bags_s[pl.ds(start + b, 1), :]
        return carry

    lax.fori_loop(0, feats, place, 0)
    send_ref[...] = rows_s[...].astype(BF16)


def scatter_kernel(cap, kind, by, after_ref, ids_ref, grad_ref, *refs):
    del after_ref
    out_ref, bags_s = refs[-2:]
    rows = out_ref.shape[0]
    first = lax.rem(lax.axis_index("dp") + by, lax.axis_size("dp")) * rows
    tile = min(rows, 512)
    lines = ids_ref.shape[0] // 2
    step = 4 if lines % 4 == 0 else 1
    one, zero = jnp.ones((), BF16), jnp.zeros((), BF16)
    at = (iota((tile, LANES), 0) + 1).astype(I16)
    for source in range(bags_s.shape[0] // cap):
        start = (2 * source + kind) * cap
        bags_s[source * cap : (source + 1) * cap, :] = grad_ref[start : start + cap, :]

    def part(r, carry):
        base = first + r * tile
        here = pl.ds(pl.multiple_of(r * tile, tile), tile)
        total = jnp.zeros((tile, LANES), F32) if len(refs) == 2 else refs[0][here, :]
        for k in range(0, lines, step):
            counts = []
            for line in range(k, k + step):
                a = jnp.broadcast_to(ids_ref[line : line + 1, :] - base, (tile, LANES)).astype(I16)
                b = jnp.broadcast_to(
                    ids_ref[lines + line : lines + line + 1, :] - base, (tile, LANES)
                ).astype(I16)
                counts.append(jnp.where(a == at, one, zero) + jnp.where(b == at, one, zero))
            total = total + dot(
                jnp.concatenate(counts, axis=1), bags_s[k * LANES : (k + step) * LANES, :]
            )
        out_ref[here, :] = total.astype(out_ref.dtype)
        return carry

    lax.fori_loop(0, rows // tile, part, 0)


def call(kernel, outs, ins, scratch=()):
    return pl.pallas_call(
        kernel,
        out_shape=outs,
        in_specs=ins,
        out_specs=jax.tree.map(lambda _: VMEM, outs),
        scratch_shapes=list(scratch),
        compiler_params=params,
    )


def in_hbm(x):
    return pltpu.with_memory_space_constraint(x, pltpu.HBM)


def in_vmem(x):
    return pltpu.with_memory_space_constraint(x, pltpu.VMEM)


def shape(dims, dtype):
    return jax.ShapeDtypeStruct(dims, dtype)


def body(
    emb_table,
    versions,
    conf_local,
    conf_version,
    conf_values,
    owners,
    row_local,
    lengths,
    dense_out,
    labels,
    cross_down,
    cross_up,
    cross_bias,
    head_weight,
):
    peers, replicas = lax.axis_size("table"), lax.axis_size("dp")
    half = peers // 2
    groups = [list(range(half)), list(range(half, peers))]
    rows_dev, width = emb_table.shape
    samples, feats, slots = row_local.shape
    cap = round_up(3 * samples * feats // (2 * peers), 16)
    chunks = -(-cap // LANES)
    per = round_up(slots * chunks, 8)
    lines_half = half * cap // LANES
    wide = cross_down.shape[1]
    own_rows = rows_dev // replicas

    def shift(x, by):
        if by == 0:
            return x
        return lax.ppermute(x, "dp", [(i, (i + by) % replicas) for i in range(replicas)])

    def across(x):
        return lax.ppermute(x, "table", [(i, (i + half) % peers) for i in range(peers)])

    def exchange(x):
        return lax.all_to_all(
            x, "table", split_axis=0, concat_axis=0, axis_index_groups=groups, tiled=True
        )

    down = [shift(cross_down[0], by) for by in range(replicas)]
    up = [shift(cross_up[0], by) for by in range(replicas)]

    position, requests = call(
        functools.partial(route_kernel, peers, cap),
        (shape((feats, samples), I32), shape((peers * per, LANES), I32)),
        [VMEM] * 3,
        [pltpu.VMEM((round_up(feats, 8), samples), I32)] * 3
        + [
            pltpu.VMEM((2 * peers * per, feats * samples), BF16),
            pltpu.VMEM((LANES, feats * samples), BF16),
        ],
    )(*map(in_hbm, (owners.transpose(1, 2, 0), row_local.transpose(1, 2, 0), lengths.T)))
    asked = exchange(requests.reshape(half, 2 * per, LANES)).reshape(2 * half * per, LANES)
    table, part = call(
        update_kernel,
        (shape((rows_dev, 2 * width), BF16), shape((own_rows, width), BF16)),
        [ANY] + [SMEM] * 3 + [VMEM] * 2,
        [pltpu.VMEM((rows_dev + 8, width), F32)],
    )(requests, *map(in_hbm, (conf_local, conf_version, versions, emb_table, conf_values)))
    part = across(part)
    part, asked = lax.optimization_barrier((part, asked))
    mirror = [shift(part, by) for by in range(replicas)]

    group = max(g for g in range(1, half + 1) if half % g == 0 and g * cap <= 2 * 320)

    def lookup(kind, tables, filled=()):
        rows = sum(t.shape[0] for t in tables)
        return pl.pallas_call(
            functools.partial(lookup_kernel, kind, half, cap),
            out_shape=shape((peers * cap, width), BF16),
            in_specs=[VMEM] + [ANY] * len(filled) + [VMEM] * len(tables),
            out_specs=ANY,
            scratch_shapes=[
                pltpu.VMEM((2, group * cap, rows), BF16),
                pltpu.VMEM((half * cap, width), BF16),
                pltpu.SemaphoreType.DMA((half,)),
            ],
            input_output_aliases={1: 0} if filled else {},
            compiler_params=params,
        )(asked, *filled, *tables)

    found = lookup(0, [table])
    found = lookup(1, mirror, (found,))
    answer = exchange(found.reshape(half, 2 * cap, width)).reshape(peers * cap, width)
    answer = in_vmem(answer)

    logits, send = call(
        functools.partial(dense_kernel, replicas),
        (shape((1, samples), F32), shape((peers * cap, width), BF16)),
        [SMEM] + [VMEM] * 3 + [ANY] * (2 * replicas) + [VMEM] * 2,
        [
            pltpu.VMEM((peers * cap, width), F32),
            pltpu.VMEM((samples, wide), BF16),
            pltpu.VMEM((samples, wide), F32),
            pltpu.VMEM((samples * feats, width), F32),
            pltpu.VMEM((replicas,) + down[0].shape, BF16),
            pltpu.VMEM((replicas,) + up[0].shape, BF16),
            pltpu.SemaphoreType.DMA((2 * replicas,)),
        ],
    )(
        position,
        answer,
        dense_out,
        labels.reshape(1, samples),
        *map(in_hbm, down),
        *map(in_hbm, up),
        cross_bias,
        head_weight.reshape(1, wide),
    )
    asked = asked.reshape(half, 2, per, LANES)
    got = exchange(send.reshape(half, 2 * cap, width)).reshape(peers * cap, width)
    got = in_vmem(got)

    def scatter(kind, by, after, init=()):
        lines = jnp.concatenate(
            [
                asked[:, kind, slot * chunks : (slot + 1) * chunks]
                .reshape(half, chunks * LANES)[:, :cap]
                .reshape(lines_half, LANES)
                for slot in range(slots)
            ]
        )
        return call(
            functools.partial(scatter_kernel, cap, kind, by),
            shape((own_rows, width), F32),
            [ANY] + [VMEM] * (2 + len(init)),
            [pltpu.VMEM((half * cap, width), BF16)],
        )(after, lines, got, *init)

    last = asked
    returned, total = None, None
    for by in range(1, replicas):
        last = scatter(1, by, last)
        part = shift(last, by)
        returned = part if returned is None else returned + part
    last = scatter(1, 0, last)
    last = (last if returned is None else returned + last).astype(BF16)
    returned = across(last)
    for by in range(1, replicas):
        last = scatter(0, by, last)
        part = shift(last, by)
        total = part if total is None else total + part
    total = scatter(0, 0, last, () if total is None else (total,))
    grads = total + returned.astype(F32)
    return (logits.reshape(samples), grads)


def solution(mesh):
    in_specs = (
        P("table", None),
        P("table"),
        P("table"),
        P("table"),
        P("table", None),
        P(("table", "dp"), None, None),
        P(("table", "dp"), None, None),
        P(("table", "dp"), None),
        P(("table", "dp"), None),
        P(("table", "dp")),
        P(None, None, "dp"),
        P(None, "dp", None),
        P(),
        P(),
    )
    out_specs = (P(("table", "dp")), P(("table", "dp"), None))
    return jax.shard_map(body, mesh=mesh, in_specs=in_specs, out_specs=out_specs, check_vma=False)
```

```python
import functools

import jax
import jax.numpy as jnp
from jax import lax
from jax.experimental import pallas as pl
from jax.experimental.pallas import tpu as pltpu
from jax.sharding import PartitionSpec as P

loss_scale = 64.0
LANES = 128
F32, BF16, I32, I16 = jnp.float32, jnp.bfloat16, jnp.int32, jnp.int16
VMEM = pl.BlockSpec(memory_space=pltpu.VMEM)
SMEM = pl.BlockSpec(memory_space=pltpu.SMEM)
ANY = pl.BlockSpec(memory_space=pl.ANY)
params = pltpu.CompilerParams(vmem_limit_bytes=36 * 1024 * 1024)
NT = (((1,), (1,)), ((), ()))


def dot(a, b, dims=(((1,), (0,)), ((), ()))):
    return lax.dot_general(a, b, dims, preferred_element_type=F32)


def iota(shape, axis):
    return lax.broadcasted_iota(I32, shape, axis)


def round_up(value, step):
    return -(-value // step) * step


def route_kernel(
    peers, cap, after_ref, owner_ref, rows_ref, len_ref, pos_ref, req_ref, own_s, one_s, two_s, a_s, b_s
):
    del after_ref
    feats, lanes = len_ref.shape
    padded = own_s.shape[0]
    chunks = -(-cap // LANES)
    half = peers // 2
    per = req_ref.shape[0] // peers
    count = peers * per
    own_s[...] = jnp.full(own_s.shape, -1, I32)
    for f in range(feats):
        own_s[f : f + 1, :] = owner_ref[f]
        one_s[f : f + 1, :] = rows_ref[f, 0:1, :]
        two_s[f : f + 1, :] = rows_ref[f, 1:2, :]
    own = own_s[...]
    hits = [(own == o).astype(F32) for o in range(peers)]
    stacked = jnp.concatenate(hits, axis=0).astype(BF16)
    row, col = iota((lanes, 2 * lanes), 0), iota((lanes, 2 * lanes), 1)
    upper = jnp.where((row < col) | (col >= lanes), 1.0, 0.0).astype(BF16)
    sums = dot(stacked, upper)
    totals = jnp.concatenate(
        [sums[o * padded : (o + 1) * padded, lanes:] for o in range(peers)], axis=1
    ).astype(BF16)
    lower = jnp.where(iota((padded, padded), 1) < iota((padded, padded), 0), 1.0, 0.0).astype(BF16)
    base = dot(lower, totals)
    rank = jnp.zeros((padded, lanes), F32)
    for o in range(peers):
        before = sums[o * padded : (o + 1) * padded, :lanes] + base[:, o * lanes : (o + 1) * lanes]
        rank = rank + hits[o] * before
    rank = rank.astype(I32)
    far = own >= half
    column = jnp.where(far, own - half, own)
    side = (lax.axis_index("table") >= half).astype(I32)
    mirrored = jnp.where(far, 1 - side, side)
    place = jnp.where(own < 0, -8, column * 2 + mirrored)
    pos_ref[...] = (place * cap + rank)[0:feats, :]
    first = place * per + lax.shift_right_logical(rank, 7)
    second = first + chunks
    low = rank & (LANES - 1)
    lengths = len_ref[...]
    one = jnp.where(lengths > 0, one_s[0:feats, :] + 1, 0)
    two = jnp.where(lengths > 1, two_s[0:feats, :] + 1, 0)
    at = iota((count, lanes), 0)
    lane_at = iota((LANES, lanes), 0)
    for f in range(feats):
        held = jnp.where(at == first[f : f + 1, :], one[f : f + 1, :], 0)
        held = jnp.where(at == second[f : f + 1, :], two[f : f + 1, :], held)
        span = slice(f * lanes, (f + 1) * lanes)
        a_s[0:count, span] = lax.shift_right_logical(held, 7).astype(F32).astype(BF16)
        a_s[count : 2 * count, span] = (held & 127).astype(F32).astype(BF16)
        b_s[:, span] = jnp.where(lane_at == low[f : f + 1, :], 1.0, 0.0).astype(BF16)
    found = dot(a_s[...], b_s[...], NT)
    req_ref[...] = (found[0:count] * 128.0 + found[count:]).astype(I32)


def update_kernel(
    local_ref, new_ref, versions_ref, table_ref, values_ref, table_out_ref, part_ref, rows_s
):
    held_rows, width = table_ref.shape
    rows_s[0:held_rows, :] = table_ref[...]

    def entry(i, carry):
        at = local_ref[i]
        to = jnp.where(new_ref[i] > versions_ref[at], at, held_rows)
        rows_s[pl.ds(to, 1), :] = values_ref[pl.ds(i, 1), :]
        return carry

    lax.fori_loop(0, values_ref.shape[0], entry, 0, unroll=8)
    table = rows_s[0:held_rows, :]
    high = table.astype(BF16)
    table_out_ref[:, 0:width] = high
    table_out_ref[:, width:] = (table - high.astype(F32)).astype(BF16)
    own_rows = part_ref.shape[0]
    start = pl.multiple_of(lax.axis_index("dp") * own_rows, own_rows)
    part_ref[...] = rows_s[pl.ds(start, own_rows), :].astype(BF16)


def lookup_kernel(peers, cap, partners, pieces, after_ref, ids_ref, table_ref, *refs):
    del after_ref
    mirror, outs, count_s = refs[:pieces], refs[pieces:-1], refs[-1]
    width = outs[0].shape[1]
    per = ids_ref.shape[0] // (2 * peers)
    chunks = -(-cap // LANES)
    one, zero = jnp.ones((), BF16), jnp.zeros((), BF16)
    at_dp = lax.axis_index("dp")
    at_table = lax.rem(lax.axis_index("table"), peers)
    own_rows = mirror[0].shape[0]
    bases = [lax.rem(at_dp + pieces - p, pieces) * own_rows for p in range(pieces)]
    spans = [[(0, table_ref.shape[0])], [(base, own_rows) for base in bases]]

    def count(kind):
        for g, partner in enumerate(partners):
            start = ((at_table ^ partner) * 2 + kind) * per
            block = ids_ref[pl.ds(pl.multiple_of(start, 8), per), :].T
            for c in range(chunks):
                n = min(LANES, cap - c * LANES)
                at = g * cap + c * LANES
                a = jnp.broadcast_to(block[0:n, c : c + 1], (n, LANES))
                b = jnp.broadcast_to(block[0:n, chunks + c : chunks + c + 1], (n, LANES))
                column = 0
                for base, rows in spans[kind]:
                    a16, b16 = (a - base).astype(I16), (b - base).astype(I16)
                    for k in range(0, rows, LANES):
                        size = min(LANES, rows - k)
                        row = (iota((n, size), 1) + (1 + k)).astype(I16)
                        count_s[kind, at : at + n, column : column + size] = jnp.where(
                            a16[:, :size] == row, one, zero
                        ) + jnp.where(b16[:, :size] == row, one, zero)
                        column += size

    def give(kind, found):
        for g, out in enumerate(outs):
            out[kind * cap : (kind + 1) * cap, :] = found[g * cap : (g + 1) * cap, :].astype(BF16)

    count(0)
    count(1)
    both = dot(count_s[0], table_ref[...])
    give(0, both[:, 0:width] + both[:, width:])
    found = dot(count_s[1, :, 0:own_rows], mirror[0][...])
    for p in range(1, pieces):
        found = found + dot(count_s[1, :, p * own_rows : (p + 1) * own_rows], mirror[p][...])
    give(1, found)


def dense_kernel(pieces, partners, cap, *refs):
    answers, refs = refs[:partners], refs[partners:]
    pos_ref, dense_ref, labels_ref = refs[0:3]
    bias_ref, head_ref, logit_ref = refs[3 + 2 * pieces : 6 + 2 * pieces]
    send_ref, rows_s, x_s, factor_s, bags_s, down_s, up_s, sems = refs[6 + 2 * pieces :]
    at_table = lax.rem(lax.axis_index("table"), partners)
    load_down = pltpu.make_async_copy(refs[3], down_s, sems.at[0])
    load_up = pltpu.make_async_copy(refs[3 + pieces], up_s, sems.at[1])
    load_down.start()
    load_up.start()
    down = (down_s,) + refs[4 : 3 + pieces]
    up = (up_s,) + refs[4 + pieces : 3 + 2 * pieces]
    feats, samples = pos_ref.shape
    width = dense_ref.shape[1]
    for p, answer in enumerate(answers):
        at = pl.multiple_of((at_table ^ p) * 2 * cap, 16)
        rows_s[pl.ds(at, 2 * cap), :] = answer[...].astype(F32)

    def fetch(f, carry):
        start = f * samples
        for b in range(samples):
            bags_s[pl.ds(start + b, 1), :] = rows_s[pl.ds(pos_ref[f, b], 1), :]
        return carry

    lax.fori_loop(0, feats, fetch, 0)
    x_s[:, 0:width] = dense_ref[...]
    for f in range(feats):
        x_s[:, (f + 1) * width : (f + 2) * width] = bags_s[
            f * samples : (f + 1) * samples, :
        ].astype(BF16)
    rows_s[...] = jnp.zeros(rows_s.shape, F32)
    load_down.wait()
    x = x_s[...]
    crossed = [dot(x, w[...]).astype(BF16) for w in down]
    load_up.wait()
    total = jnp.zeros((samples, width), F32)
    blocks = feats + 1
    for k in range(blocks):
        span = slice(k * width, (k + 1) * width)
        factor = bias_ref[:, span]
        for c, w in zip(crossed, up):
            factor = factor + dot(c, w[:, span])
        factor_s[:, span] = factor
        base = x_s[:, span].astype(F32)
        total = total + (base * factor + base) * head_ref[:, span]
    logits = jnp.sum(total, axis=1, keepdims=True)
    logit_ref[...] = jnp.broadcast_to(logits, (samples, samples)).T[0:1, :]
    labels = jnp.broadcast_to(labels_ref[...].astype(F32), (samples, samples)).T[:, 0:1]
    signal = loss_scale * (jax.nn.sigmoid(logits) - labels)
    lifts = []
    for k in range(blocks):
        span = slice(k * width, (k + 1) * width)
        lifts.append(((signal * head_ref[:, span]) * x_s[:, span].astype(F32)).astype(BF16))
    lift = jnp.concatenate(lifts, axis=1)
    back = [dot(lift, w[...], NT).astype(BF16) for w in up]
    for f in range(feats):
        span = slice((f + 1) * width, (f + 2) * width)
        outer = signal * head_ref[:, span]
        grad = outer
        for c, w in zip(back, down):
            grad = grad + dot(c, w[span, :], NT)
        bags_s[f * samples : (f + 1) * samples, :] = grad + outer * factor_s[:, span]

    def place(f, carry):
        start = f * samples
        for b in range(samples):
            rows_s[pl.ds(pos_ref[f, b], 1), :] = bags_s[pl.ds(start + b, 1), :]
        return carry

    lax.fori_loop(0, feats, place, 0)
    send_ref[...] = rows_s[...].astype(BF16)


def scatter_kernel(cap, kind, by, replicas, after_ref, *refs):
    del after_ref
    ids, grads, (out_ref, bags_s) = refs[:replicas], refs[replicas:-2], refs[-2:]
    rows = out_ref.shape[0]
    tile = min(rows, 512)
    each = ids[0].shape[0] // 2
    slots = each * LANES
    step = 4 if each % 4 == 0 else 1
    one, zero = jnp.ones((), BF16), jnp.zeros((), BF16)
    at = (iota((tile, LANES), 0) + 1).astype(I16)
    for r, grad in enumerate(grads):
        for source in range(slots // cap):
            start = (2 * source + kind) * cap
            to = r * slots + source * cap
            bags_s[to : to + cap, :] = grad[start : start + cap, :]
    first = lax.rem(lax.axis_index("dp") + by, lax.axis_size("dp")) * rows
    for start in range(0, rows, tile):
        base = first + start
        total = jnp.zeros((tile, LANES), F32)
        for r, lines in enumerate(ids):
            for k in range(0, each, step):
                counts = []
                for line in range(k, k + step):
                    a = lines[line : line + 1, :] - base
                    b = lines[each + line : each + line + 1, :] - base
                    a = jnp.broadcast_to(a, (tile, LANES)).astype(I16)
                    b = jnp.broadcast_to(b, (tile, LANES)).astype(I16)
                    counts.append(jnp.where(a == at, one, zero) + jnp.where(b == at, one, zero))
                here = r * slots + k * LANES
                total = total + dot(
                    jnp.concatenate(counts, axis=1), bags_s[here : here + step * LANES, :]
                )
        out_ref[start : start + tile, :] = total


def call(kernel, outs, ins, scratch=(), flops=0, moved=0):
    cost = pl.CostEstimate(flops=flops, bytes_accessed=moved, transcendentals=0)
    return pl.pallas_call(
        kernel,
        out_shape=outs,
        in_specs=ins,
        out_specs=jax.tree.map(lambda _: VMEM, outs),
        scratch_shapes=list(scratch),
        compiler_params=params,
        cost_estimate=cost,
    )


def in_hbm(x):
    return pltpu.with_memory_space_constraint(x, pltpu.HBM)


def in_vmem(x):
    return pltpu.with_memory_space_constraint(x, pltpu.VMEM)


def shape(dims, dtype):
    return jax.ShapeDtypeStruct(dims, dtype)


def body(
    emb_table,
    versions,
    conf_local,
    conf_version,
    conf_values,
    owners,
    row_local,
    lengths,
    dense_out,
    labels,
    cross_down,
    cross_up,
    cross_bias,
    head_weight,
):
    peers, replicas = lax.axis_size("table"), lax.axis_size("dp")
    half = peers // 2
    groups = [list(range(half)), list(range(half, peers))]
    rows_dev, width = emb_table.shape
    samples, feats, slots = row_local.shape
    cap = round_up(3 * samples * feats // (2 * peers), 16)
    chunks = -(-cap // LANES)
    per = round_up(slots * chunks, 8)
    lines_half = half * cap // LANES
    wide = cross_down.shape[1]
    own_rows = rows_dev // replicas

    def shift(x, by):
        if by == 0:
            return x
        return lax.ppermute(x, "dp", [(i, (i + by) % replicas) for i in range(replicas)])

    def across(x):
        return lax.ppermute(x, "table", [(i, (i + half) % peers) for i in range(peers)])

    def exchange(x):
        return lax.all_to_all(
            x, "table", split_axis=0, concat_axis=0, axis_index_groups=groups, tiled=True
        )

    down = [shift(cross_down[0], by) for by in range(replicas)]
    up = [shift(cross_up[0], by) for by in range(replicas)]

    table, part = call(
        update_kernel,
        (shape((rows_dev, 2 * width), BF16), shape((own_rows, width), BF16)),
        [SMEM] * 3 + [VMEM] * 2,
        [pltpu.VMEM((rows_dev + 8, width), F32)],
    )(*map(in_hbm, (conf_local, conf_version, versions, emb_table, conf_values)))
    position, requests = call(
        functools.partial(route_kernel, peers, cap),
        (shape((feats, samples), I32), shape((peers * per, LANES), I32)),
        [ANY] + [VMEM] * 3,
        [pltpu.VMEM((round_up(feats, 8), samples), I32)] * 3
        + [
            pltpu.VMEM((2 * peers * per, feats * samples), BF16),
            pltpu.VMEM((LANES, feats * samples), BF16),
        ],
    )(part, *map(in_hbm, (owners.transpose(1, 2, 0), row_local.transpose(1, 2, 0), lengths.T)))
    asked = exchange(requests.reshape(half, 2 * per, LANES)).reshape(2 * half * per, LANES)
    part = across(part)
    part, asked = lax.optimization_barrier((part, asked))
    mirror = [shift(part, by) for by in range(replicas)]

    def meet(x, partner):
        if partner == 0:
            return x
        return lax.ppermute(x, "table", [(i, i ^ partner) for i in range(peers)])

    steps = 4 if half % 8 == 0 else 1
    pairs = [(i, half - 1 - i) for i in range(half // 2, half)]
    group = len(pairs) // steps
    answers = [None] * half
    after = [asked, asked]
    for start in range(len(pairs) - group, -1, -group):
        partners = [p for pair in pairs[start : start + group] for p in pair]
        found = call(
            functools.partial(lookup_kernel, half, cap, partners, replicas),
            tuple(shape((2 * cap, width), BF16) for _ in partners),
            [ANY] + [VMEM] * (2 + replicas),
            [pltpu.VMEM((2, 2 * group * cap, rows_dev), BF16)],
        )(after[-2], asked, table, *mirror)
        for partner, sums in zip(partners, found):
            answers[partner] = meet(sums, partner)
        after.append(answers[partners[0]])

    logits, send = call(
        functools.partial(dense_kernel, replicas, half, cap),
        (shape((1, samples), F32), shape((peers * cap, width), BF16)),
        [VMEM] * half + [SMEM] + [VMEM] * 2 + ([ANY] + [VMEM] * (replicas - 1)) * 2 + [VMEM] * 2,
        [
            pltpu.VMEM((peers * cap, width), F32),
            pltpu.VMEM((samples, wide), BF16),
            pltpu.VMEM((samples, wide), F32),
            pltpu.VMEM((samples * feats, width), F32),
            pltpu.VMEM(down[0].shape, BF16),
            pltpu.VMEM(up[0].shape, BF16),
            pltpu.SemaphoreType.DMA((2,)),
        ],
    )(
        *map(in_vmem, answers),
        position,
        dense_out,
        labels.reshape(1, samples),
        in_hbm(down[0]),
        *map(in_vmem, down[1:]),
        in_hbm(up[0]),
        *map(in_vmem, up[1:]),
        cross_bias,
        head_weight.reshape(1, wide),
    )
    ids = asked.reshape(half, 2, per, LANES)
    got = in_vmem(exchange(send.reshape(half, 2 * cap, width)).reshape(peers * cap, width))

    def lines_of(kind):
        return jnp.concatenate(
            [
                ids[:, kind, slot * chunks : (slot + 1) * chunks]
                .reshape(half, chunks * LANES)[:, :cap]
                .reshape(lines_half, LANES)
                for slot in range(slots)
            ]
        )

    def scatter(kind, by, after, lines, grads):
        return call(
            functools.partial(scatter_kernel, cap, kind, by, len(lines)),
            shape((own_rows, width), F32),
            [ANY] + [VMEM] * (2 * len(lines)),
            [pltpu.VMEM((len(lines) * half * cap, width), BF16)],
        )(after, *lines, *grads)

    mirror_lines, native_lines = lines_of(1), lines_of(0)
    last, parts = asked, []
    for by in range(1, replicas):
        last = scatter(1, by, last, [mirror_lines], [got])
        parts.append(shift(last, by))
    own = scatter(1, 0, last, [mirror_lines], [got])
    mirrored = functools.reduce(jnp.add, [own] + parts).astype(BF16)
    returned = across(mirrored)
    every_line = [shift(native_lines, by) for by in range(replicas)]
    every_got = [in_vmem(shift(got, by)) for by in range(replicas)]
    grads = scatter(0, 0, mirrored, every_line, every_got) + returned.astype(F32)
    return (logits.reshape(samples), grads)


def solution(mesh):
    in_specs = (
        P("table", None),
        P("table"),
        P("table"),
        P("table"),
        P("table", None),
        P(("table", "dp"), None, None),
        P(("table", "dp"), None, None),
        P(("table", "dp"), None),
        P(("table", "dp"), None),
        P(("table", "dp")),
        P(None, None, "dp"),
        P(None, "dp", None),
        P(),
        P(),
    )
    out_specs = (P(("table", "dp")), P(("table", "dp"), None))
    return jax.shard_map(body, mesh=mesh, in_specs=in_specs, out_specs=out_specs, check_vma=False)
```

```python
import functools

import jax
import jax.numpy as jnp
from jax import lax
from jax.experimental import pallas as pl
from jax.experimental.pallas import tpu as pltpu
from jax.sharding import PartitionSpec as P

loss_scale = 64.0
LANES = 128
F32, BF16, I32, I16 = jnp.float32, jnp.bfloat16, jnp.int32, jnp.int16
VMEM = pl.BlockSpec(memory_space=pltpu.VMEM)
SMEM = pl.BlockSpec(memory_space=pltpu.SMEM)
ANY = pl.BlockSpec(memory_space=pl.ANY)
params = pltpu.CompilerParams(vmem_limit_bytes=36 * 1024 * 1024)
NT = (((1,), (1,)), ((), ()))


def dot(a, b, dims=(((1,), (0,)), ((), ()))):
    return lax.dot_general(a, b, dims, preferred_element_type=F32)


def iota(shape, axis):
    return lax.broadcasted_iota(I32, shape, axis)


def round_up(value, step):
    return -(-value // step) * step


def route_kernel(
    peers, cap, after_ref, owner_ref, rows_ref, len_ref, pos_ref, req_ref, own_s, one_s, two_s, a_s, b_s
):
    del after_ref
    feats, lanes = len_ref.shape
    padded = own_s.shape[0]
    chunks = -(-cap // LANES)
    half = peers // 2
    per = req_ref.shape[0] // peers
    count = peers * per
    own_s[...] = jnp.full(own_s.shape, -1, I32)
    for f in range(feats):
        own_s[f : f + 1, :] = owner_ref[f]
        one_s[f : f + 1, :] = rows_ref[f, 0:1, :]
        two_s[f : f + 1, :] = rows_ref[f, 1:2, :]
    own = own_s[...]
    hits = [(own == o).astype(F32) for o in range(peers)]
    stacked = jnp.concatenate(hits, axis=0).astype(BF16)
    row, col = iota((lanes, 2 * lanes), 0), iota((lanes, 2 * lanes), 1)
    upper = jnp.where((row < col) | (col >= lanes), 1.0, 0.0).astype(BF16)
    sums = dot(stacked, upper)
    totals = jnp.concatenate(
        [sums[o * padded : (o + 1) * padded, lanes:] for o in range(peers)], axis=1
    ).astype(BF16)
    lower = jnp.where(iota((padded, padded), 1) < iota((padded, padded), 0), 1.0, 0.0).astype(BF16)
    base = dot(lower, totals)
    rank = jnp.zeros((padded, lanes), F32)
    for o in range(peers):
        before = sums[o * padded : (o + 1) * padded, :lanes] + base[:, o * lanes : (o + 1) * lanes]
        rank = rank + hits[o] * before
    rank = rank.astype(I32)
    far = own >= half
    column = jnp.where(far, own - half, own)
    side = (lax.axis_index("table") >= half).astype(I32)
    mirrored = jnp.where(far, 1 - side, side)
    place = jnp.where(own < 0, -8, column * 2 + mirrored)
    pos_ref[...] = ((mirrored * half + column) * cap + rank)[0:feats, :]
    first = place * per + lax.shift_right_logical(rank, 7)
    second = first + chunks
    low = rank & (LANES - 1)
    lengths = len_ref[...]
    one = jnp.where(lengths > 0, one_s[0:feats, :] + 1, 0)
    two = jnp.where(lengths > 1, two_s[0:feats, :] + 1, 0)
    at = iota((count, lanes), 0)
    lane_at = iota((LANES, lanes), 0)
    for f in range(feats):
        held = jnp.where(at == first[f : f + 1, :], one[f : f + 1, :], 0)
        held = jnp.where(at == second[f : f + 1, :], two[f : f + 1, :], held)
        span = slice(f * lanes, (f + 1) * lanes)
        a_s[0:count, span] = lax.shift_right_logical(held, 7).astype(F32).astype(BF16)
        a_s[count : 2 * count, span] = (held & 127).astype(F32).astype(BF16)
        b_s[:, span] = jnp.where(lane_at == low[f : f + 1, :], 1.0, 0.0).astype(BF16)
    found = dot(a_s[...], b_s[...], NT)
    req_ref[...] = (found[0:count] * 128.0 + found[count:]).astype(I32)


def update_kernel(
    local_ref, new_ref, versions_ref, table_ref, values_ref, table_out_ref, part_ref, rows_s
):
    held_rows, width = table_ref.shape
    rows_s[0:held_rows, :] = table_ref[...]

    def entry(i, carry):
        at = local_ref[i]
        to = jnp.where(new_ref[i] > versions_ref[at], at, held_rows)
        rows_s[pl.ds(to, 1), :] = values_ref[pl.ds(i, 1), :]
        return carry

    lax.fori_loop(0, values_ref.shape[0], entry, 0, unroll=8)
    table = rows_s[0:held_rows, :]
    high = table.astype(BF16)
    table_out_ref[:, 0:width] = high
    table_out_ref[:, width:] = (table - high.astype(F32)).astype(BF16)
    own_rows = part_ref.shape[0]
    start = pl.multiple_of(lax.axis_index("dp") * own_rows, own_rows)
    part_ref[...] = rows_s[pl.ds(start, own_rows), :].astype(BF16)


def lookup_kernel(peers, cap, partners, pieces, after_ref, ids_ref, table_ref, *refs):
    del after_ref
    mirror, outs, count_s = refs[:pieces], refs[pieces:-1], refs[-1]
    width = outs[0].shape[1]
    per = ids_ref.shape[0] // (2 * peers)
    chunks = -(-cap // LANES)
    one, zero = jnp.ones((), BF16), jnp.zeros((), BF16)
    at_dp = lax.axis_index("dp")
    at_table = lax.rem(lax.axis_index("table"), peers)
    own_rows = mirror[0].shape[0]
    bases = [lax.rem(at_dp + pieces - p, pieces) * own_rows for p in range(pieces)]
    spans = [[(0, table_ref.shape[0])], [(base, own_rows) for base in bases]]

    def count(kind):
        for g, partner in enumerate(partners):
            start = ((at_table ^ partner) * 2 + kind) * per
            block = ids_ref[pl.ds(pl.multiple_of(start, 8), per), :].T
            for c in range(chunks):
                n = min(LANES, cap - c * LANES)
                at = g * cap + c * LANES
                a = jnp.broadcast_to(block[0:n, c : c + 1], (n, LANES))
                b = jnp.broadcast_to(block[0:n, chunks + c : chunks + c + 1], (n, LANES))
                column = 0
                for base, rows in spans[kind]:
                    a16, b16 = (a - base).astype(I16), (b - base).astype(I16)
                    for k in range(0, rows, LANES):
                        size = min(LANES, rows - k)
                        row = (iota((n, size), 1) + (1 + k)).astype(I16)
                        count_s[kind, at : at + n, column : column + size] = jnp.where(
                            a16[:, :size] == row, one, zero
                        ) + jnp.where(b16[:, :size] == row, one, zero)
                        column += size

    def give(kind, found):
        for g, out in enumerate(outs):
            out[kind * cap : (kind + 1) * cap, :] = found[g * cap : (g + 1) * cap, :].astype(BF16)

    count(0)
    count(1)
    both = dot(count_s[0], table_ref[...])
    give(0, both[:, 0:width] + both[:, width:])
    found = dot(count_s[1, :, 0:own_rows], mirror[0][...])
    for p in range(1, pieces):
        found = found + dot(count_s[1, :, p * own_rows : (p + 1) * own_rows], mirror[p][...])
    give(1, found)


def dense_kernel(pieces, partners, cap, *refs):
    answers, refs = refs[:partners], refs[partners:]
    pos_ref, dense_ref, labels_ref = refs[0:3]
    bias_ref, head_ref, logit_ref = refs[3 + 2 * pieces : 6 + 2 * pieces]
    native_ref, mirror_ref, rows_s, x_s, factor_s, bags_s, down_s, up_s, sems = refs[
        6 + 2 * pieces :
    ]
    at_table = lax.rem(lax.axis_index("table"), partners)
    load_down = pltpu.make_async_copy(refs[3], down_s, sems.at[0])
    load_up = pltpu.make_async_copy(refs[3 + pieces], up_s, sems.at[1])
    load_down.start()
    load_up.start()
    down = (down_s,) + refs[4 : 3 + pieces]
    up = (up_s,) + refs[4 + pieces : 3 + 2 * pieces]
    feats, samples = pos_ref.shape
    width = dense_ref.shape[1]
    for p, answer in enumerate(answers):
        for kind in range(2):
            at = pl.multiple_of((kind * partners + (at_table ^ p)) * cap, 16)
            rows_s[pl.ds(at, cap), :] = answer[kind * cap : (kind + 1) * cap, :].astype(F32)

    def fetch(f, carry):
        start = f * samples
        for b in range(samples):
            bags_s[pl.ds(start + b, 1), :] = rows_s[pl.ds(pos_ref[f, b], 1), :]
        return carry

    lax.fori_loop(0, feats, fetch, 0)
    x_s[:, 0:width] = dense_ref[...]
    for f in range(feats):
        x_s[:, (f + 1) * width : (f + 2) * width] = bags_s[
            f * samples : (f + 1) * samples, :
        ].astype(BF16)
    load_down.wait()
    x = x_s[...]
    crossed = [dot(x, w[...]).astype(BF16) for w in down]
    load_up.wait()
    total = jnp.zeros((samples, width), F32)
    blocks = feats + 1
    for k in range(blocks):
        span = slice(k * width, (k + 1) * width)
        factor = bias_ref[:, span]
        for c, w in zip(crossed, up):
            factor = factor + dot(c, w[:, span])
        factor_s[:, span] = factor
        base = x_s[:, span].astype(F32)
        total = total + (base * factor + base) * head_ref[:, span]
    logits = jnp.sum(total, axis=1, keepdims=True)
    logit_ref[...] = jnp.broadcast_to(logits, (samples, samples)).T[0:1, :]
    labels = jnp.broadcast_to(labels_ref[...].astype(F32), (samples, samples)).T[:, 0:1]
    signal = loss_scale * (jax.nn.sigmoid(logits) - labels)
    lifts = []
    for k in range(blocks):
        span = slice(k * width, (k + 1) * width)
        lifts.append(((signal * head_ref[:, span]) * x_s[:, span].astype(F32)).astype(BF16))
    lift = jnp.concatenate(lifts, axis=1)
    back = [dot(lift, w[...], NT).astype(BF16) for w in up]
    for f in range(feats):
        span = slice((f + 1) * width, (f + 2) * width)
        outer = signal * head_ref[:, span]
        grad = outer
        for c, w in zip(back, down):
            grad = grad + dot(c, w[span, :], NT)
        bags_s[f * samples : (f + 1) * samples, :] = grad + outer * factor_s[:, span]

    def place(f, carry):
        start = f * samples
        for b in range(samples):
            rows_s[pl.ds(pos_ref[f, b], 1), :] = bags_s[pl.ds(start + b, 1), :]
        return carry

    lax.fori_loop(0, feats, place, 0)
    native_ref[...] = rows_s[0 : partners * cap, :].astype(BF16)
    mirror_ref[...] = rows_s[partners * cap :, :].astype(BF16)


def scatter_kernel(by, replicas, after_ref, *refs):
    del after_ref
    ids, grads, (out_ref, bags_s) = refs[:replicas], refs[replicas:-2], refs[-2:]
    rows = out_ref.shape[0]
    tile = min(rows, 512)
    each = ids[0].shape[0] // 2
    slots = each * LANES
    step = 4 if each % 4 == 0 else 1
    one, zero = jnp.ones((), BF16), jnp.zeros((), BF16)
    at = (iota((tile, LANES), 0) + 1).astype(I16)
    start = 0
    for grad in grads:
        bags_s[start : start + grad.shape[0], :] = grad[...]
        start += grad.shape[0]
    first = lax.rem(lax.axis_index("dp") + by, lax.axis_size("dp")) * rows
    for start in range(0, rows, tile):
        base = first + start
        total = jnp.zeros((tile, LANES), F32)
        for r, lines in enumerate(ids):
            for k in range(0, each, step):
                counts = []
                for line in range(k, k + step):
                    a = lines[line : line + 1, :] - base
                    b = lines[each + line : each + line + 1, :] - base
                    a = jnp.broadcast_to(a, (tile, LANES)).astype(I16)
                    b = jnp.broadcast_to(b, (tile, LANES)).astype(I16)
                    counts.append(jnp.where(a == at, one, zero) + jnp.where(b == at, one, zero))
                here = r * slots + k * LANES
                total = total + dot(
                    jnp.concatenate(counts, axis=1), bags_s[here : here + step * LANES, :]
                )
        out_ref[start : start + tile, :] = total


def call(kernel, outs, ins, scratch=(), flops=1024, moved=1024):
    cost = pl.CostEstimate(flops=flops, bytes_accessed=moved, transcendentals=0)
    return pl.pallas_call(
        kernel,
        out_shape=outs,
        in_specs=ins,
        out_specs=jax.tree.map(lambda _: VMEM, outs),
        scratch_shapes=list(scratch),
        compiler_params=params,
        cost_estimate=cost,
    )


def in_hbm(x):
    return pltpu.with_memory_space_constraint(x, pltpu.HBM)


def in_vmem(x):
    return pltpu.with_memory_space_constraint(x, pltpu.VMEM)


def shape(dims, dtype):
    return jax.ShapeDtypeStruct(dims, dtype)


def body(
    emb_table,
    versions,
    conf_local,
    conf_version,
    conf_values,
    owners,
    row_local,
    lengths,
    dense_out,
    labels,
    cross_down,
    cross_up,
    cross_bias,
    head_weight,
):
    peers, replicas = lax.axis_size("table"), lax.axis_size("dp")
    half = peers // 2
    groups = [list(range(half)), list(range(half, peers))]
    rows_dev, width = emb_table.shape
    samples, feats, slots = row_local.shape
    cap = round_up(3 * samples * feats // (2 * peers), 16)
    chunks = -(-cap // LANES)
    per = round_up(slots * chunks, 8)
    lines_half = half * cap // LANES
    wide = cross_down.shape[1]
    own_rows = rows_dev // replicas

    def shift(x, by):
        if by == 0:
            return x
        return lax.ppermute(x, "dp", [(i, (i + by) % replicas) for i in range(replicas)])

    def across(x):
        return lax.ppermute(x, "table", [(i, (i + half) % peers) for i in range(peers)])

    def exchange(x):
        return lax.all_to_all(
            x, "table", split_axis=0, concat_axis=0, axis_index_groups=groups, tiled=True
        )


    table, part = call(
        update_kernel,
        (shape((rows_dev, 2 * width), BF16), shape((own_rows, width), BF16)),
        [SMEM] * 3 + [VMEM] * 2,
        [pltpu.VMEM((rows_dev + 8, width), F32)],
    )(*map(in_hbm, (conf_local, conf_version, versions, emb_table, conf_values)))
    position, requests = call(
        functools.partial(route_kernel, peers, cap),
        (shape((feats, samples), I32), shape((peers * per, LANES), I32)),
        [ANY] + [VMEM] * 3,
        [pltpu.VMEM((round_up(feats, 8), samples), I32)] * 3
        + [
            pltpu.VMEM((2 * peers * per, feats * samples), BF16),
            pltpu.VMEM((LANES, feats * samples), BF16),
        ],
    )(part, *map(in_hbm, (owners.transpose(1, 2, 0), row_local.transpose(1, 2, 0), lengths.T)))
    down = [shift(cross_down[0], by) for by in range(replicas)]
    up = [shift(cross_up[0], by) for by in range(replicas)]
    asked = exchange(requests.reshape(half, 2 * per, LANES)).reshape(2 * half * per, LANES)
    part = across(part)
    part, asked = lax.optimization_barrier((part, asked))
    mirror = [shift(part, by) for by in range(replicas)]
    asked, down, up = lax.optimization_barrier((asked, down, up))

    def meet(x, partner):
        if partner == 0:
            return x
        return lax.ppermute(x, "table", [(i, i ^ partner) for i in range(peers)])

    steps = 4 if half % 8 == 0 else 1
    pairs = [(i, half - 1 - i) for i in range(half // 2, half)]
    group = len(pairs) // steps
    answers = [None] * half
    after = [asked, asked]
    for start in range(len(pairs) - group, -1, -group):
        partners = [p for pair in pairs[start : start + group] for p in pair]
        found = call(
            functools.partial(lookup_kernel, half, cap, partners, replicas),
            tuple(shape((2 * cap, width), BF16) for _ in partners),
            [ANY] + [VMEM] * (2 + replicas),
            [pltpu.VMEM((2, 2 * group * cap, rows_dev), BF16)],
        )(after[-2], asked, table, *mirror)
        for partner, sums in zip(partners, found):
            answers[partner] = meet(sums, partner)
        after.append(answers[partners[0]])

    logits, to_native, to_mirror = call(
        functools.partial(dense_kernel, replicas, half, cap),
        (shape((1, samples), F32),) + (shape((half * cap, width), BF16),) * 2,
        [VMEM] * half + [SMEM] + [VMEM] * 2 + ([ANY] + [VMEM] * (replicas - 1)) * 2 + [VMEM] * 2,
        [
            pltpu.VMEM((peers * cap, width), F32),
            pltpu.VMEM((samples, wide), BF16),
            pltpu.VMEM((samples, wide), F32),
            pltpu.VMEM((samples * feats, width), F32),
            pltpu.VMEM(down[0].shape, BF16),
            pltpu.VMEM(up[0].shape, BF16),
            pltpu.SemaphoreType.DMA((2,)),
        ],
    )(
        *map(in_vmem, answers),
        position,
        dense_out,
        labels.reshape(1, samples),
        in_hbm(down[0]),
        *map(in_vmem, down[1:]),
        in_hbm(up[0]),
        *map(in_vmem, up[1:]),
        cross_bias,
        head_weight.reshape(1, wide),
    )
    ids = asked.reshape(half, 2, per, LANES)
    got_mirror = exchange(to_mirror.reshape(half, cap, width)).reshape(half * cap, width)
    got_mirror, to_native = lax.optimization_barrier((got_mirror, to_native))
    got_native = exchange(to_native.reshape(half, cap, width)).reshape(half * cap, width)
    whole_native = got_native
    got_mirror, got_native = in_vmem(got_mirror), in_vmem(got_native)

    def lines_of(kind):
        return jnp.concatenate(
            [
                ids[:, kind, slot * chunks : (slot + 1) * chunks]
                .reshape(half, chunks * LANES)[:, :cap]
                .reshape(lines_half, LANES)
                for slot in range(slots)
            ]
        )

    def scatter(by, after, lines, grads):
        return call(
            functools.partial(scatter_kernel, by, len(lines)),
            shape((own_rows, width), F32),
            [ANY] + [VMEM] * (len(lines) + len(grads)),
            [pltpu.VMEM((len(lines) * half * cap, width), BF16)],
        )(after, *lines, *grads)

    mirror_lines, native_lines = lines_of(1), lines_of(0)
    last, parts = asked, []
    for by in range(1, replicas):
        last = scatter(by, last, [mirror_lines], [got_mirror])
        parts.append(shift(last, by))
    own = scatter(0, last, [mirror_lines], [got_mirror])
    mirrored = functools.reduce(jnp.add, [own] + parts).astype(BF16)
    returned = across(mirrored)
    every_line = [shift(native_lines, by) for by in range(replicas)]
    pieces = 4 if half * cap % 64 == 0 else 1
    size = half * cap // pieces
    every_got = [got_native]
    for by in range(1, replicas):
        for i in range(pieces):
            every_got.append(in_vmem(shift(whole_native[i * size : (i + 1) * size], by)))
    grads = scatter(0, mirrored, every_line, every_got) + returned.astype(F32)
    return (logits.reshape(samples), grads)


def solution(mesh):
    in_specs = (
        P("table", None),
        P("table"),
        P("table"),
        P("table"),
        P("table", None),
        P(("table", "dp"), None, None),
        P(("table", "dp"), None, None),
        P(("table", "dp"), None),
        P(("table", "dp"), None),
        P(("table", "dp")),
        P(None, None, "dp"),
        P(None, "dp", None),
        P(),
        P(),
    )
    out_specs = (P(("table", "dp")), P(("table", "dp"), None))
    return jax.shard_map(body, mesh=mesh, in_specs=in_specs, out_specs=out_specs, check_vma=False)
```

```python
import functools

import jax
import jax.numpy as jnp
from jax import lax
from jax.experimental import pallas as pl
from jax.experimental.pallas import tpu as pltpu
from jax.sharding import PartitionSpec as P

loss_scale = 64.0
LANES = 128
F32, BF16, I32, I16 = jnp.float32, jnp.bfloat16, jnp.int32, jnp.int16
VMEM = pl.BlockSpec(memory_space=pltpu.VMEM)
SMEM = pl.BlockSpec(memory_space=pltpu.SMEM)
ANY = pl.BlockSpec(memory_space=pl.ANY)
params = pltpu.CompilerParams(vmem_limit_bytes=36 * 1024 * 1024)
NT = (((1,), (1,)), ((), ()))


def dot(a, b, dims=(((1,), (0,)), ((), ()))):
    return lax.dot_general(a, b, dims, preferred_element_type=F32)


def iota(shape, axis):
    return lax.broadcasted_iota(I32, shape, axis)


def round_up(value, step):
    return -(-value // step) * step


def route_kernel(
    peers, cap, after_ref, owner_ref, rows_ref, len_ref, pos_ref, req_ref, own_s, one_s, two_s, a_s, b_s
):
    del after_ref
    feats, lanes = len_ref.shape
    padded = own_s.shape[0]
    chunks = -(-cap // LANES)
    half = peers // 2
    per = req_ref.shape[0] // peers
    count = peers * per
    own_s[...] = jnp.full(own_s.shape, -1, I32)
    for f in range(feats):
        own_s[f : f + 1, :] = owner_ref[f]
        one_s[f : f + 1, :] = rows_ref[f, 0:1, :]
        two_s[f : f + 1, :] = rows_ref[f, 1:2, :]
    own = own_s[...]
    hits = [(own == o).astype(F32) for o in range(peers)]
    stacked = jnp.concatenate(hits, axis=0).astype(BF16)
    row, col = iota((lanes, 2 * lanes), 0), iota((lanes, 2 * lanes), 1)
    upper = jnp.where((row < col) | (col >= lanes), 1.0, 0.0).astype(BF16)
    sums = dot(stacked, upper)
    totals = jnp.concatenate(
        [sums[o * padded : (o + 1) * padded, lanes:] for o in range(peers)], axis=1
    ).astype(BF16)
    lower = jnp.where(iota((padded, padded), 1) < iota((padded, padded), 0), 1.0, 0.0).astype(BF16)
    base = dot(lower, totals)
    rank = jnp.zeros((padded, lanes), F32)
    for o in range(peers):
        before = sums[o * padded : (o + 1) * padded, :lanes] + base[:, o * lanes : (o + 1) * lanes]
        rank = rank + hits[o] * before
    rank = rank.astype(I32)
    far = own >= half
    column = jnp.where(far, own - half, own)
    side = (lax.axis_index("table") >= half).astype(I32)
    mirrored = jnp.where(far, 1 - side, side)
    place = jnp.where(own < 0, -8, column * 2 + mirrored)
    pos_ref[...] = ((mirrored * half + column) * cap + rank)[0:feats, :]
    first = place * per + lax.shift_right_logical(rank, 7)
    second = first + chunks
    low = rank & (LANES - 1)
    lengths = len_ref[...]
    one = jnp.where(lengths > 0, one_s[0:feats, :] + 1, 0)
    two = jnp.where(lengths > 1, two_s[0:feats, :] + 1, 0)
    at = iota((count, lanes), 0)
    lane_at = iota((LANES, lanes), 0)
    for f in range(feats):
        held = jnp.where(at == first[f : f + 1, :], one[f : f + 1, :], 0)
        held = jnp.where(at == second[f : f + 1, :], two[f : f + 1, :], held)
        span = slice(f * lanes, (f + 1) * lanes)
        a_s[0:count, span] = lax.shift_right_logical(held, 7).astype(F32).astype(BF16)
        a_s[count : 2 * count, span] = (held & 127).astype(F32).astype(BF16)
        b_s[:, span] = jnp.where(lane_at == low[f : f + 1, :], 1.0, 0.0).astype(BF16)
    found = dot(a_s[...], b_s[...], NT)
    req_ref[...] = (found[0:count] * 128.0 + found[count:]).astype(I32)


def update_kernel(
    local_ref, new_ref, versions_ref, table_ref, values_ref, table_out_ref, part_ref, rows_s
):
    held_rows, width = table_ref.shape
    rows_s[0:held_rows, :] = table_ref[...]

    def entry(i, carry):
        at = local_ref[i]
        to = jnp.where(new_ref[i] > versions_ref[at], at, held_rows)
        rows_s[pl.ds(to, 1), :] = values_ref[pl.ds(i, 1), :]
        return carry

    lax.fori_loop(0, values_ref.shape[0], entry, 0, unroll=8)
    table = rows_s[0:held_rows, :]
    high = table.astype(BF16)
    table_out_ref[:, 0:width] = high
    table_out_ref[:, width:] = (table - high.astype(F32)).astype(BF16)
    own_rows = part_ref.shape[0]
    start = pl.multiple_of(lax.axis_index("dp") * own_rows, own_rows)
    part_ref[...] = rows_s[pl.ds(start, own_rows), :].astype(BF16)


def lookup_kernel(peers, cap, partners, pieces, after_ref, ids_ref, table_ref, *refs):
    del after_ref
    mirror, outs, count_s = refs[:pieces], refs[pieces:-1], refs[-1]
    width = outs[0].shape[1]
    per = ids_ref.shape[0] // (2 * peers)
    chunks = -(-cap // LANES)
    one, zero = jnp.ones((), BF16), jnp.zeros((), BF16)
    at_dp = lax.axis_index("dp")
    at_table = lax.rem(lax.axis_index("table"), peers)
    own_rows = mirror[0].shape[0]
    bases = [lax.rem(at_dp + pieces - p, pieces) * own_rows for p in range(pieces)]
    spans = [[(0, table_ref.shape[0])], [(base, own_rows) for base in bases]]

    def count(kind):
        for g, partner in enumerate(partners):
            start = ((at_table ^ partner) * 2 + kind) * per
            block = ids_ref[pl.ds(pl.multiple_of(start, 8), per), :].T
            for c in range(chunks):
                n = min(LANES, cap - c * LANES)
                at = g * cap + c * LANES
                a = jnp.broadcast_to(block[0:n, c : c + 1], (n, LANES))
                b = jnp.broadcast_to(block[0:n, chunks + c : chunks + c + 1], (n, LANES))
                column = 0
                for base, rows in spans[kind]:
                    a16, b16 = (a - base).astype(I16), (b - base).astype(I16)
                    for k in range(0, rows, LANES):
                        size = min(LANES, rows - k)
                        row = (iota((n, size), 1) + (1 + k)).astype(I16)
                        count_s[kind, at : at + n, column : column + size] = jnp.where(
                            a16[:, :size] == row, one, zero
                        ) + jnp.where(b16[:, :size] == row, one, zero)
                        column += size

    def give(kind, found):
        for g, out in enumerate(outs):
            out[kind * cap : (kind + 1) * cap, :] = found[g * cap : (g + 1) * cap, :].astype(BF16)

    count(0)
    count(1)
    both = dot(count_s[0], table_ref[...])
    give(0, both[:, 0:width] + both[:, width:])
    found = dot(count_s[1, :, 0:own_rows], mirror[0][...])
    for p in range(1, pieces):
        found = found + dot(count_s[1, :, p * own_rows : (p + 1) * own_rows], mirror[p][...])
    give(1, found)


def dense_kernel(pieces, partners, cap, *refs):
    answers, refs = refs[:partners], refs[partners:]
    pos_ref, dense_ref, labels_ref = refs[0:3]
    bias_ref, head_ref, logit_ref = refs[3 + 2 * pieces : 6 + 2 * pieces]
    native_ref, mirror_ref, rows_s, x_s, factor_s, bags_s, down_s, up_s, sems = refs[
        6 + 2 * pieces :
    ]
    at_table = lax.rem(lax.axis_index("table"), partners)
    load_down = pltpu.make_async_copy(refs[3], down_s, sems.at[0])
    load_up = pltpu.make_async_copy(refs[3 + pieces], up_s, sems.at[1])
    load_down.start()
    load_up.start()
    down = (down_s,) + refs[4 : 3 + pieces]
    up = (up_s,) + refs[4 + pieces : 3 + 2 * pieces]
    feats, samples = pos_ref.shape
    width = dense_ref.shape[1]
    for p, answer in enumerate(answers):
        for kind in range(2):
            at = pl.multiple_of((kind * partners + (at_table ^ p)) * cap, 16)
            rows_s[pl.ds(at, cap), :] = answer[kind * cap : (kind + 1) * cap, :].astype(F32)

    def fetch(f, carry):
        start = f * samples
        for b in range(samples):
            bags_s[pl.ds(start + b, 1), :] = rows_s[pl.ds(pos_ref[f, b], 1), :]
        return carry

    lax.fori_loop(0, feats, fetch, 0)
    x_s[:, 0:width] = dense_ref[...]
    for f in range(feats):
        x_s[:, (f + 1) * width : (f + 2) * width] = bags_s[
            f * samples : (f + 1) * samples, :
        ].astype(BF16)
    load_down.wait()
    x = x_s[...]
    crossed = [dot(x, w[...]).astype(BF16) for w in down]
    load_up.wait()
    total = jnp.zeros((samples, width), F32)
    wide = x_s.shape[1]
    step = 2 * width
    spans = [slice(k, min(k + step, wide)) for k in range(0, wide, step)]
    for span in spans:
        factor = bias_ref[:, span]
        for c, w in zip(crossed, up):
            factor = factor + dot(c, w[:, span])
        factor_s[:, span] = factor
        base = x_s[:, span].astype(F32)
        terms = (base * factor + base) * head_ref[:, span]
        for k in range(0, terms.shape[1], width):
            total = total + terms[:, k : k + width]
    logits = jnp.sum(total, axis=1, keepdims=True)
    logit_ref[...] = jnp.broadcast_to(logits, (samples, samples)).T[0:1, :]
    labels = jnp.broadcast_to(labels_ref[...].astype(F32), (samples, samples)).T[:, 0:1]
    signal = loss_scale * (jax.nn.sigmoid(logits) - labels)
    lifts = []
    for span in spans:
        lifts.append(((signal * head_ref[:, span]) * x_s[:, span].astype(F32)).astype(BF16))
    lift = jnp.concatenate(lifts, axis=1)
    back = [dot(lift, w[...], NT).astype(BF16) for w in up]
    for start in range(width, wide, step):
        span = slice(start, min(start + step, wide))
        outer = signal * head_ref[:, span]
        grad = outer
        for c, w in zip(back, down):
            grad = grad + dot(c, w[span, :], NT)
        grad = grad + outer * factor_s[:, span]
        for k in range(0, grad.shape[1], width):
            f = (start + k) // width - 1
            bags_s[f * samples : (f + 1) * samples, :] = grad[:, k : k + width]

    def place(f, carry):
        start = f * samples
        for b in range(samples):
            rows_s[pl.ds(pos_ref[f, b], 1), :] = bags_s[pl.ds(start + b, 1), :]
        return carry

    lax.fori_loop(0, feats, place, 0)
    native_ref[...] = rows_s[0 : partners * cap, :].astype(BF16)
    mirror_ref[...] = rows_s[partners * cap :, :].astype(BF16)


def scatter_kernel(by, replicas, after_ref, *refs):
    del after_ref
    ids, grads, (out_ref, bags_s) = refs[:replicas], refs[replicas:-2], refs[-2:]
    rows = out_ref.shape[0]
    tile = min(rows, 512)
    each = ids[0].shape[0] // 2
    slots = each * LANES
    step = 4 if each % 4 == 0 else 1
    one, zero = jnp.ones((), BF16), jnp.zeros((), BF16)
    at = (iota((tile, LANES), 0) + 1).astype(I16)
    start = 0
    for grad in grads:
        bags_s[start : start + grad.shape[0], :] = grad[...]
        start += grad.shape[0]
    first = lax.rem(lax.axis_index("dp") + by, lax.axis_size("dp")) * rows
    for start in range(0, rows, tile):
        base = first + start
        total = jnp.zeros((tile, LANES), F32)
        for r, lines in enumerate(ids):
            for k in range(0, each, step):
                counts = []
                for line in range(k, k + step):
                    a = lines[line : line + 1, :] - base
                    b = lines[each + line : each + line + 1, :] - base
                    a = jnp.broadcast_to(a, (tile, LANES)).astype(I16)
                    b = jnp.broadcast_to(b, (tile, LANES)).astype(I16)
                    counts.append(jnp.where(a == at, one, zero) + jnp.where(b == at, one, zero))
                here = r * slots + k * LANES
                total = total + dot(
                    jnp.concatenate(counts, axis=1), bags_s[here : here + step * LANES, :]
                )
        out_ref[start : start + tile, :] = total


def call(kernel, outs, ins, scratch=(), flops=1024, moved=1024):
    cost = pl.CostEstimate(flops=flops, bytes_accessed=moved, transcendentals=0)
    return pl.pallas_call(
        kernel,
        out_shape=outs,
        in_specs=ins,
        out_specs=jax.tree.map(lambda _: VMEM, outs),
        scratch_shapes=list(scratch),
        compiler_params=params,
        cost_estimate=cost,
    )


def in_hbm(x):
    return pltpu.with_memory_space_constraint(x, pltpu.HBM)


def in_vmem(x):
    return pltpu.with_memory_space_constraint(x, pltpu.VMEM)


def shape(dims, dtype):
    return jax.ShapeDtypeStruct(dims, dtype)


def body(
    emb_table,
    versions,
    conf_local,
    conf_version,
    conf_values,
    owners,
    row_local,
    lengths,
    dense_out,
    labels,
    cross_down,
    cross_up,
    cross_bias,
    head_weight,
):
    peers, replicas = lax.axis_size("table"), lax.axis_size("dp")
    half = peers // 2
    groups = [list(range(half)), list(range(half, peers))]
    rows_dev, width = emb_table.shape
    samples, feats, slots = row_local.shape
    cap = round_up(3 * samples * feats // (2 * peers), 16)
    chunks = -(-cap // LANES)
    per = round_up(slots * chunks, 8)
    lines_half = half * cap // LANES
    wide = cross_down.shape[1]
    own_rows = rows_dev // replicas

    def shift(x, by):
        if by == 0:
            return x
        return lax.ppermute(x, "dp", [(i, (i + by) % replicas) for i in range(replicas)])

    def across(x):
        return lax.ppermute(x, "table", [(i, (i + half) % peers) for i in range(peers)])

    def exchange(x):
        return lax.all_to_all(
            x, "table", split_axis=0, concat_axis=0, axis_index_groups=groups, tiled=True
        )


    table, part = call(
        update_kernel,
        (shape((rows_dev, 2 * width), BF16), shape((own_rows, width), BF16)),
        [SMEM] * 3 + [VMEM] * 2,
        [pltpu.VMEM((rows_dev + 8, width), F32)],
    )(*map(in_hbm, (conf_local, conf_version, versions, emb_table, conf_values)))
    position, requests = call(
        functools.partial(route_kernel, peers, cap),
        (shape((feats, samples), I32), shape((peers * per, LANES), I32)),
        [ANY] + [VMEM] * 3,
        [pltpu.VMEM((round_up(feats, 8), samples), I32)] * 3
        + [
            pltpu.VMEM((2 * peers * per, feats * samples), BF16),
            pltpu.VMEM((LANES, feats * samples), BF16),
        ],
    )(part, *map(in_hbm, (owners.transpose(1, 2, 0), row_local.transpose(1, 2, 0), lengths.T)))
    down = [shift(cross_down[0], by) for by in range(replicas)]
    up = [shift(cross_up[0], by) for by in range(replicas)]
    asked = exchange(requests.reshape(half, 2 * per, LANES)).reshape(2 * half * per, LANES)
    part = across(part)
    part, asked = lax.optimization_barrier((part, asked))
    mirror = [shift(part, by) for by in range(replicas)]
    asked, down, up = lax.optimization_barrier((asked, down, up))

    def meet(x, partner):
        if partner == 0:
            return x
        return lax.ppermute(x, "table", [(i, i ^ partner) for i in range(peers)])

    steps = 4 if half % 8 == 0 else 1
    pairs = [(i, half - 1 - i) for i in range(half // 2, half)]
    group = len(pairs) // steps
    answers = [None] * half
    after = [asked, asked, asked]
    for start in range(len(pairs) - group, -1, -group):
        partners = [p for pair in pairs[start : start + group] for p in pair]
        found = call(
            functools.partial(lookup_kernel, half, cap, partners, replicas),
            tuple(shape((2 * cap, width), BF16) for _ in partners),
            [ANY] + [VMEM] * (2 + replicas),
            [pltpu.VMEM((2, 2 * group * cap, rows_dev), BF16)],
        )(after[-3], asked, table, *mirror)
        for partner, sums in zip(partners, found):
            answers[partner] = meet(sums, partner)
        after.append(answers[partners[0]])

    logits, to_native, to_mirror = call(
        functools.partial(dense_kernel, replicas, half, cap),
        (shape((1, samples), F32),) + (shape((half * cap, width), BF16),) * 2,
        [VMEM] * half + [SMEM] + [VMEM] * 2 + ([ANY] + [VMEM] * (replicas - 1)) * 2 + [VMEM] * 2,
        [
            pltpu.VMEM((peers * cap, width), F32),
            pltpu.VMEM((samples, wide), BF16),
            pltpu.VMEM((samples, wide), F32),
            pltpu.VMEM((samples * feats, width), F32),
            pltpu.VMEM(down[0].shape, BF16),
            pltpu.VMEM(up[0].shape, BF16),
            pltpu.SemaphoreType.DMA((2,)),
        ],
    )(
        *map(in_vmem, answers),
        position,
        dense_out,
        labels.reshape(1, samples),
        in_hbm(down[0]),
        *map(in_vmem, down[1:]),
        in_hbm(up[0]),
        *map(in_vmem, up[1:]),
        cross_bias,
        head_weight.reshape(1, wide),
    )
    ids = asked.reshape(half, 2, per, LANES)
    got_mirror = exchange(to_mirror.reshape(half, cap, width)).reshape(half * cap, width)
    got_mirror, to_native = lax.optimization_barrier((got_mirror, to_native))
    got_native = exchange(to_native.reshape(half, cap, width)).reshape(half * cap, width)
    whole_native = got_native
    got_mirror, got_native = in_vmem(got_mirror), in_vmem(got_native)

    def lines_of(kind):
        return jnp.concatenate(
            [
                ids[:, kind, slot * chunks : (slot + 1) * chunks]
                .reshape(half, chunks * LANES)[:, :cap]
                .reshape(lines_half, LANES)
                for slot in range(slots)
            ]
        )

    def scatter(by, after, lines, grads):
        return call(
            functools.partial(scatter_kernel, by, len(lines)),
            shape((own_rows, width), F32),
            [ANY] + [VMEM] * (len(lines) + len(grads)),
            [pltpu.VMEM((len(lines) * half * cap, width), BF16)],
        )(after, *lines, *grads)

    mirror_lines, native_lines = lines_of(1), lines_of(0)
    last, parts = asked, []
    for by in range(1, replicas):
        last = scatter(by, last, [mirror_lines], [got_mirror])
        parts.append(shift(last, by))
    own = scatter(0, last, [mirror_lines], [got_mirror])
    mirrored = functools.reduce(jnp.add, [own] + parts).astype(BF16)
    returned = across(mirrored)
    every_line = [shift(native_lines, by) for by in range(replicas)]
    pieces = 4 if half * cap % 64 == 0 else 1
    size = half * cap // pieces
    every_got = [got_native]
    for by in range(1, replicas):
        for i in range(pieces):
            every_got.append(in_vmem(shift(whole_native[i * size : (i + 1) * size], by)))
    grads = scatter(0, mirrored, every_line, every_got) + returned.astype(F32)
    return (logits.reshape(samples), grads)


def solution(mesh):
    in_specs = (
        P("table", None),
        P("table"),
        P("table"),
        P("table"),
        P("table", None),
        P(("table", "dp"), None, None),
        P(("table", "dp"), None, None),
        P(("table", "dp"), None),
        P(("table", "dp"), None),
        P(("table", "dp")),
        P(None, None, "dp"),
        P(None, "dp", None),
        P(),
        P(),
    )
    out_specs = (P(("table", "dp")), P(("table", "dp"), None))
    return jax.shard_map(body, mesh=mesh, in_specs=in_specs, out_specs=out_specs, check_vma=False)
```

```python
import functools

import jax
import jax.numpy as jnp
from jax import lax
from jax.experimental import pallas as pl
from jax.experimental.pallas import tpu as pltpu
from jax.sharding import PartitionSpec as P

loss_scale = 64.0
LANES = 128
F32, BF16, I32, I16 = jnp.float32, jnp.bfloat16, jnp.int32, jnp.int16
VMEM = pl.BlockSpec(memory_space=pltpu.VMEM)
SMEM = pl.BlockSpec(memory_space=pltpu.SMEM)
ANY = pl.BlockSpec(memory_space=pl.ANY)
params = pltpu.CompilerParams(vmem_limit_bytes=36 * 1024 * 1024)
NT = (((1,), (1,)), ((), ()))


def dot(a, b, dims=(((1,), (0,)), ((), ()))):
    return lax.dot_general(a, b, dims, preferred_element_type=F32)


def iota(shape, axis):
    return lax.broadcasted_iota(I32, shape, axis)


def round_up(value, step):
    return -(-value // step) * step


def route_kernel(
    peers, cap, table_ref, owner_ref, rows_ref, len_ref, pos_ref, req_ref, table_out_ref, own_s, one_s, two_s, a_s, b_s
):
    held_rows, width = table_out_ref.shape[0], table_ref.shape[1]
    table = table_ref[0:held_rows, :]
    high = table.astype(BF16)
    table_out_ref[:, 0:width] = high
    table_out_ref[:, width:] = (table - high.astype(F32)).astype(BF16)
    feats, lanes = len_ref.shape
    padded = own_s.shape[0]
    chunks = -(-cap // LANES)
    half = peers // 2
    per = req_ref.shape[0] // peers
    count = peers * per
    own_s[...] = jnp.full(own_s.shape, -1, I32)
    for f in range(feats):
        own_s[f : f + 1, :] = owner_ref[f]
        one_s[f : f + 1, :] = rows_ref[f, 0:1, :]
        two_s[f : f + 1, :] = rows_ref[f, 1:2, :]
    own = own_s[...]
    hits = [(own == o).astype(F32) for o in range(peers)]
    stacked = jnp.concatenate(hits, axis=0).astype(BF16)
    row, col = iota((lanes, 2 * lanes), 0), iota((lanes, 2 * lanes), 1)
    upper = jnp.where((row < col) | (col >= lanes), 1.0, 0.0).astype(BF16)
    sums = dot(stacked, upper)
    totals = jnp.concatenate(
        [sums[o * padded : (o + 1) * padded, lanes:] for o in range(peers)], axis=1
    ).astype(BF16)
    lower = jnp.where(iota((padded, padded), 1) < iota((padded, padded), 0), 1.0, 0.0).astype(BF16)
    base = dot(lower, totals)
    rank = jnp.zeros((padded, lanes), F32)
    for o in range(peers):
        before = sums[o * padded : (o + 1) * padded, :lanes] + base[:, o * lanes : (o + 1) * lanes]
        rank = rank + hits[o] * before
    rank = rank.astype(I32)
    far = own >= half
    column = jnp.where(far, own - half, own)
    side = (lax.axis_index("table") >= half).astype(I32)
    mirrored = jnp.where(far, 1 - side, side)
    column = jnp.where(mirrored > 0, column ^ (half // 2), column)
    place = jnp.where(own < 0, -8, column * 2 + mirrored)
    pos_ref[...] = ((mirrored * half + column) * cap + rank)[0:feats, :]
    first = place * per + lax.shift_right_logical(rank, 7)
    second = first + chunks
    low = rank & (LANES - 1)
    lengths = len_ref[...]
    one = jnp.where(lengths > 0, one_s[0:feats, :] + 1, 0)
    two = jnp.where(lengths > 1, two_s[0:feats, :] + 1, 0)
    at = iota((count, lanes), 0)
    lane_at = iota((LANES, lanes), 0)
    for f in range(feats):
        held = jnp.where(at == first[f : f + 1, :], one[f : f + 1, :], 0)
        held = jnp.where(at == second[f : f + 1, :], two[f : f + 1, :], held)
        span = slice(f * lanes, (f + 1) * lanes)
        a_s[0:count, span] = lax.shift_right_logical(held, 7).astype(F32).astype(BF16)
        a_s[count : 2 * count, span] = (held & 127).astype(F32).astype(BF16)
        b_s[:, span] = jnp.where(lane_at == low[f : f + 1, :], 1.0, 0.0).astype(BF16)
    found = dot(a_s[...], b_s[...], NT)
    req_ref[...] = (found[0:count] * 128.0 + found[count:]).astype(I32)


def update_kernel(
    local_ref, new_ref, versions_ref, table_ref, values_ref, rows_s, part_ref
):
    held_rows, width = table_ref.shape
    rows_s[0:held_rows, :] = table_ref[...]

    def entry(i, carry):
        at = local_ref[i]
        to = jnp.where(new_ref[i] > versions_ref[at], at, held_rows)
        rows_s[pl.ds(to, 1), :] = values_ref[pl.ds(i, 1), :]
        return carry

    lax.fori_loop(0, values_ref.shape[0], entry, 0, unroll=32)
    own_rows = part_ref.shape[0]
    start = pl.multiple_of(lax.axis_index("dp") * own_rows, own_rows)
    part_ref[...] = rows_s[pl.ds(start, own_rows), :].astype(BF16)


def lookup_kernel(peers, cap, partners, pieces, after_ref, ids_ref, table_ref, *refs):
    del after_ref
    mirror, outs, count_s = refs[:pieces], refs[pieces:-1], refs[-1]
    width = outs[0].shape[1]
    per = ids_ref.shape[0] // (2 * peers)
    chunks = -(-cap // LANES)
    one, zero = jnp.ones((), BF16), jnp.zeros((), BF16)
    at_dp = lax.axis_index("dp")
    at_table = lax.rem(lax.axis_index("table"), peers)
    own_rows = mirror[0].shape[0]
    bases = [lax.rem(at_dp + pieces - p, pieces) * own_rows for p in range(pieces)]
    spans = [[(0, table_ref.shape[0])], [(base, own_rows) for base in bases]]

    def count(kind):
        for g, partner in enumerate(partners):
            start = ((at_table ^ partner) * 2 + kind) * per
            block = ids_ref[pl.ds(pl.multiple_of(start, 8), per), :].T
            for c in range(chunks):
                n = min(LANES, cap - c * LANES)
                at = g * cap + c * LANES
                a = jnp.broadcast_to(block[0:n, c : c + 1], (n, LANES))
                b = jnp.broadcast_to(block[0:n, chunks + c : chunks + c + 1], (n, LANES))
                column = 0
                for base, rows in spans[kind]:
                    a16, b16 = (a - base).astype(I16), (b - base).astype(I16)
                    for k in range(0, rows, LANES):
                        size = min(LANES, rows - k)
                        row = (iota((n, size), 1) + (1 + k)).astype(I16)
                        count_s[kind, at : at + n, column : column + size] = jnp.where(
                            a16[:, :size] == row, one, zero
                        ) + jnp.where(b16[:, :size] == row, one, zero)
                        column += size

    def give(kind, found):
        for g, out in enumerate(outs):
            out[kind * cap : (kind + 1) * cap, :] = found[g * cap : (g + 1) * cap, :].astype(BF16)

    count(0)
    count(1)
    both = dot(count_s[0], table_ref[...])
    give(0, both[:, 0:width] + both[:, width:])
    found = dot(count_s[1, :, 0:own_rows], mirror[0][...])
    for p in range(1, pieces):
        found = found + dot(count_s[1, :, p * own_rows : (p + 1) * own_rows], mirror[p][...])
    give(1, found)


def dense_kernel(pieces, partners, cap, *refs):
    answers, refs = refs[:partners], refs[partners:]
    pos_ref, dense_ref, labels_ref = refs[0:3]
    bias_ref, head_ref, logit_ref = refs[3 + 2 * pieces : 6 + 2 * pieces]
    native_ref, mirror_ref, rows_s, x_s, factor_s, bags_s, down_s, up_s, sems = refs[
        6 + 2 * pieces :
    ]
    at_table = lax.rem(lax.axis_index("table"), partners)
    load_down = pltpu.make_async_copy(refs[3], down_s, sems.at[0])
    load_up = pltpu.make_async_copy(refs[3 + pieces], up_s, sems.at[1])
    load_down.start()
    load_up.start()
    down = (down_s,) + refs[4 : 3 + pieces]
    up = (up_s,) + refs[4 + pieces : 3 + 2 * pieces]
    feats, samples = pos_ref.shape
    width = dense_ref.shape[1]
    for p, answer in enumerate(answers):
        for kind in range(2):
            at = pl.multiple_of((kind * partners + (at_table ^ p)) * cap, 16)
            rows_s[pl.ds(at, cap), :] = answer[kind * cap : (kind + 1) * cap, :].astype(F32)

    def fetch(f, carry):
        start = f * samples
        for b in range(samples):
            bags_s[pl.ds(start + b, 1), :] = rows_s[pl.ds(pos_ref[f, b], 1), :]
        return carry

    lax.fori_loop(0, feats, fetch, 0)
    x_s[:, 0:width] = dense_ref[...]
    for f in range(feats):
        x_s[:, (f + 1) * width : (f + 2) * width] = bags_s[
            f * samples : (f + 1) * samples, :
        ].astype(BF16)
    load_down.wait()
    x = x_s[...]
    crossed = [dot(x, w[...]).astype(BF16) for w in down]
    load_up.wait()
    total = jnp.zeros((samples, width), F32)
    wide = x_s.shape[1]
    step = 2 * width
    spans = [slice(k, min(k + step, wide)) for k in range(0, wide, step)]
    for span in spans:
        factor = bias_ref[:, span]
        for c, w in zip(crossed, up):
            factor = factor + dot(c, w[:, span])
        factor_s[:, span] = factor
        base = x_s[:, span].astype(F32)
        terms = (base * factor + base) * head_ref[:, span]
        for k in range(0, terms.shape[1], width):
            total = total + terms[:, k : k + width]
    logits = jnp.sum(total, axis=1, keepdims=True)
    logit_ref[...] = jnp.broadcast_to(logits, (samples, samples)).T[0:1, :]
    labels = jnp.broadcast_to(labels_ref[...].astype(F32), (samples, samples)).T[:, 0:1]
    signal = loss_scale * (jax.nn.sigmoid(logits) - labels)
    lifts = []
    for span in spans:
        lifts.append(((signal * head_ref[:, span]) * x_s[:, span].astype(F32)).astype(BF16))
    lift = jnp.concatenate(lifts, axis=1)
    back = [dot(w[...], lift, NT).astype(BF16) for w in up]
    for start in range(width, wide, step):
        span = slice(start, min(start + step, wide))
        outer = signal * head_ref[:, span]
        turned = 0.0
        for c, w in zip(back, down):
            turned = turned + dot(w[span, :], c)
        grad = outer + turned.T + outer * factor_s[:, span]
        for k in range(0, grad.shape[1], width):
            f = (start + k) // width - 1
            bags_s[f * samples : (f + 1) * samples, :] = grad[:, k : k + width]

    def place(f, carry):
        start = f * samples
        for b in range(samples):
            rows_s[pl.ds(pos_ref[f, b], 1), :] = bags_s[pl.ds(start + b, 1), :]
        return carry

    lax.fori_loop(0, feats, place, 0)
    native_ref[...] = rows_s[0 : partners * cap, :].astype(BF16)
    mirror_ref[...] = rows_s[partners * cap :, :].astype(BF16)


def scatter_kernel(by, replicas, after_ref, *refs):
    del after_ref
    ids, grads, (out_ref, bags_s) = refs[:replicas], refs[replicas:-2], refs[-2:]
    rows = out_ref.shape[0]
    tile = min(rows, 512)
    each = ids[0].shape[0] // 2
    slots = each * LANES
    step = 4 if each % 4 == 0 else 1
    one, zero = jnp.ones((), BF16), jnp.zeros((), BF16)
    at = (iota((tile, LANES), 0) + 1).astype(I16)
    start = 0
    for grad in grads:
        bags_s[start : start + grad.shape[0], :] = grad[...]
        start += grad.shape[0]
    first = lax.rem(lax.axis_index("dp") + by, lax.axis_size("dp")) * rows
    for start in range(0, rows, tile):
        base = first + start
        total = jnp.zeros((tile, LANES), F32)
        for r, lines in enumerate(ids):
            for k in range(0, each, step):
                counts = []
                for line in range(k, k + step):
                    a = lines[line : line + 1, :] - base
                    b = lines[each + line : each + line + 1, :] - base
                    a = jnp.broadcast_to(a, (tile, LANES)).astype(I16)
                    b = jnp.broadcast_to(b, (tile, LANES)).astype(I16)
                    counts.append(jnp.where(a == at, one, zero) + jnp.where(b == at, one, zero))
                here = r * slots + k * LANES
                total = total + dot(
                    jnp.concatenate(counts, axis=1), bags_s[here : here + step * LANES, :]
                )
        out_ref[start : start + tile, :] = total


def call(kernel, outs, ins, scratch=(), flops=1024, moved=1024):
    cost = pl.CostEstimate(flops=flops, bytes_accessed=moved, transcendentals=0)
    return pl.pallas_call(
        kernel,
        out_shape=outs,
        in_specs=ins,
        out_specs=jax.tree.map(lambda _: VMEM, outs),
        scratch_shapes=list(scratch),
        compiler_params=params,
        cost_estimate=cost,
    )


def in_hbm(x):
    return pltpu.with_memory_space_constraint(x, pltpu.HBM)


def in_vmem(x):
    return pltpu.with_memory_space_constraint(x, pltpu.VMEM)


def shape(dims, dtype):
    return jax.ShapeDtypeStruct(dims, dtype)


def body(
    emb_table,
    versions,
    conf_local,
    conf_version,
    conf_values,
    owners,
    row_local,
    lengths,
    dense_out,
    labels,
    cross_down,
    cross_up,
    cross_bias,
    head_weight,
):
    peers, replicas = lax.axis_size("table"), lax.axis_size("dp")
    half = peers // 2
    groups = [list(range(half)), list(range(half, peers))]
    rows_dev, width = emb_table.shape
    samples, feats, slots = row_local.shape
    cap = round_up(3 * samples * feats // (2 * peers), 16)
    chunks = -(-cap // LANES)
    per = round_up(slots * chunks, 8)
    lines_half = half * cap // LANES
    wide = cross_down.shape[1]
    own_rows = rows_dev // replicas

    def shift(x, by):
        if by == 0:
            return x
        return lax.ppermute(x, "dp", [(i, (i + by) % replicas) for i in range(replicas)])

    def across(x):
        far = half + half // 2
        return lax.ppermute(x, "table", [(i, i ^ far) for i in range(peers)])

    def exchange(x):
        return lax.all_to_all(
            x, "table", split_axis=0, concat_axis=0, axis_index_groups=groups, tiled=True
        )


    rows, part = call(
        update_kernel,
        (shape((rows_dev + 8, width), F32), shape((own_rows, width), BF16)),
        [SMEM] * 3 + [VMEM] * 2,
    )(*map(in_hbm, (conf_local, conf_version, versions, emb_table, conf_values)))
    position, requests, table = call(
        functools.partial(route_kernel, peers, cap),
        (
            shape((feats, samples), I32),
            shape((peers * per, LANES), I32),
            shape((rows_dev, 2 * width), BF16),
        ),
        [VMEM] * 4,
        [pltpu.VMEM((round_up(feats, 8), samples), I32)] * 3
        + [
            pltpu.VMEM((2 * peers * per, feats * samples), BF16),
            pltpu.VMEM((LANES, feats * samples), BF16),
        ],
    )(rows, *map(in_hbm, (owners.transpose(1, 2, 0), row_local.transpose(1, 2, 0), lengths.T)))
    down = [shift(cross_down[0], by) for by in range(replicas)]
    up = [shift(cross_up[0], by) for by in range(replicas)]
    asked = exchange(requests.reshape(half, 2 * per, LANES)).reshape(2 * half * per, LANES)
    part = across(part)
    part, asked = lax.optimization_barrier((part, asked))
    mirror = [shift(part, by) for by in range(replicas)]
    asked, down, up = lax.optimization_barrier((asked, down, up))

    def meet(x, partner):
        if partner == 0:
            return x
        return lax.ppermute(x, "table", [(i, i ^ partner) for i in range(peers)])

    steps = 4 if half % 8 == 0 else 1
    pairs = [(i, half - 1 - i) for i in range(half // 2, half)]
    group = len(pairs) // steps
    answers = [None] * half
    after = [asked, asked, asked]
    for start in range(len(pairs) - group, -1, -group):
        partners = [p for pair in pairs[start : start + group] for p in pair]
        found = call(
            functools.partial(lookup_kernel, half, cap, partners, replicas),
            tuple(shape((2 * cap, width), BF16) for _ in partners),
            [ANY] + [VMEM] * (2 + replicas),
            [pltpu.VMEM((2, 2 * group * cap, rows_dev), BF16)],
        )(after[-3], asked, table, *mirror)
        for partner, sums in zip(partners, found):
            answers[partner] = meet(sums, partner)
        after.append(answers[partners[0]])

    logits, to_native, to_mirror = call(
        functools.partial(dense_kernel, replicas, half, cap),
        (shape((1, samples), F32),) + (shape((half * cap, width), BF16),) * 2,
        [VMEM] * half + [SMEM] + [VMEM] * 2 + ([ANY] + [VMEM] * (replicas - 1)) * 2 + [VMEM] * 2,
        [
            pltpu.VMEM((peers * cap, width), F32),
            pltpu.VMEM((samples, wide), BF16),
            pltpu.VMEM((samples, wide), F32),
            pltpu.VMEM((samples * feats, width), F32),
            pltpu.VMEM(down[0].shape, BF16),
            pltpu.VMEM(up[0].shape, BF16),
            pltpu.SemaphoreType.DMA((2,)),
        ],
    )(
        *map(in_vmem, answers),
        position,
        dense_out,
        labels.reshape(1, samples),
        in_hbm(down[0]),
        *map(in_vmem, down[1:]),
        in_hbm(up[0]),
        *map(in_vmem, up[1:]),
        cross_bias,
        head_weight.reshape(1, wide),
    )
    ids = asked.reshape(half, 2, per, LANES)
    got_mirror = exchange(to_mirror.reshape(half, cap, width)).reshape(half * cap, width)
    got_mirror, to_native = lax.optimization_barrier((got_mirror, to_native))
    got_native = exchange(to_native.reshape(half, cap, width)).reshape(half * cap, width)
    whole_native = got_native
    got_mirror, got_native = in_vmem(got_mirror), in_vmem(got_native)

    def lines_of(kind):
        return jnp.concatenate(
            [
                ids[:, kind, slot * chunks : (slot + 1) * chunks]
                .reshape(half, chunks * LANES)[:, :cap]
                .reshape(lines_half, LANES)
                for slot in range(slots)
            ]
        )

    def scatter(by, after, lines, grads):
        return call(
            functools.partial(scatter_kernel, by, len(lines)),
            shape((own_rows, width), F32),
            [ANY] + [VMEM] * (len(lines) + len(grads)),
            [pltpu.VMEM((len(lines) * half * cap, width), BF16)],
        )(after, *lines, *grads)

    mirror_lines, native_lines = lines_of(1), lines_of(0)
    last, parts = asked, []
    for by in range(1, replicas):
        last = scatter(by, last, [mirror_lines], [got_mirror])
        parts.append(shift(last, by))
    own = scatter(0, last, [mirror_lines], [got_mirror])
    mirrored = functools.reduce(jnp.add, [own] + parts).astype(BF16)
    returned = across(mirrored)
    _, native_lines = lax.optimization_barrier((mirrored, native_lines))
    every_line = [shift(native_lines, by) for by in range(replicas)]
    pieces = 4 if half * cap % 64 == 0 else 1
    size = half * cap // pieces
    every_got = [got_native]
    for by in range(1, replicas):
        for i in range(pieces):
            every_got.append(in_vmem(shift(whole_native[i * size : (i + 1) * size], by)))
    grads = scatter(0, mirrored, every_line, every_got) + returned.astype(F32)
    return (logits.reshape(samples), grads)


def solution(mesh):
    in_specs = (
        P("table", None),
        P("table"),
        P("table"),
        P("table"),
        P("table", None),
        P(("table", "dp"), None, None),
        P(("table", "dp"), None, None),
        P(("table", "dp"), None),
        P(("table", "dp"), None),
        P(("table", "dp")),
        P(None, None, "dp"),
        P(None, "dp", None),
        P(),
        P(),
    )
    out_specs = (P(("table", "dp")), P(("table", "dp"), None))
    return jax.shard_map(body, mesh=mesh, in_specs=in_specs, out_specs=out_specs, check_vma=False)
```

```python
import functools

import jax
import jax.numpy as jnp
from jax import lax
from jax.experimental import pallas as pl
from jax.experimental.pallas import tpu as pltpu
from jax.sharding import PartitionSpec as P

loss_scale = 64.0
LANES = 128
F32, BF16, I32, I16 = jnp.float32, jnp.bfloat16, jnp.int32, jnp.int16
VMEM = pl.BlockSpec(memory_space=pltpu.VMEM)
SMEM = pl.BlockSpec(memory_space=pltpu.SMEM)
ANY = pl.BlockSpec(memory_space=pl.ANY)
params = pltpu.CompilerParams(vmem_limit_bytes=36 * 1024 * 1024)
NT = (((1,), (1,)), ((), ()))


def dot(a, b, dims=(((1,), (0,)), ((), ()))):
    return lax.dot_general(a, b, dims, preferred_element_type=F32)


def iota(shape, axis):
    return lax.broadcasted_iota(I32, shape, axis)


def round_up(value, step):
    return -(-value // step) * step


def route_kernel(
    peers, cap, table_ref, owner_ref, rows_ref, len_ref, pos_ref, req_ref, table_out_ref, own_s, one_s, two_s, a_s, b_s
):
    held_rows, width = table_out_ref.shape[0], table_ref.shape[1]
    table = table_ref[0:held_rows, :]
    high = table.astype(BF16)
    table_out_ref[:, 0:width] = high
    table_out_ref[:, width:] = (table - high.astype(F32)).astype(BF16)
    feats, lanes = len_ref.shape
    padded = own_s.shape[0]
    chunks = -(-cap // LANES)
    half = peers // 2
    per = req_ref.shape[0] // peers
    count = peers * per
    own_s[...] = jnp.full(own_s.shape, -1, I32)
    for f in range(feats):
        own_s[f : f + 1, :] = owner_ref[f]
        one_s[f : f + 1, :] = rows_ref[f, 0:1, :]
        two_s[f : f + 1, :] = rows_ref[f, 1:2, :]
    own = own_s[...]
    hits = [(own == o).astype(F32) for o in range(peers)]
    stacked = jnp.concatenate(hits, axis=0).astype(BF16)
    row, col = iota((lanes, 2 * lanes), 0), iota((lanes, 2 * lanes), 1)
    upper = jnp.where((row < col) | (col >= lanes), 1.0, 0.0).astype(BF16)
    sums = dot(stacked, upper)
    totals = jnp.concatenate(
        [sums[o * padded : (o + 1) * padded, lanes:] for o in range(peers)], axis=1
    ).astype(BF16)
    lower = jnp.where(iota((padded, padded), 1) < iota((padded, padded), 0), 1.0, 0.0).astype(BF16)
    base = dot(lower, totals)
    rank = jnp.zeros((padded, lanes), F32)
    for o in range(peers):
        before = sums[o * padded : (o + 1) * padded, :lanes] + base[:, o * lanes : (o + 1) * lanes]
        rank = rank + hits[o] * before
    rank = rank.astype(I32)
    far = own >= half
    column = jnp.where(far, own - half, own)
    side = (lax.axis_index("table") >= half).astype(I32)
    mirrored = jnp.where(far, 1 - side, side)
    column = jnp.where(mirrored > 0, column ^ (half // 2), column)
    place = jnp.where(own < 0, -8, column * 2 + mirrored)
    pos_ref[...] = ((mirrored * half + column) * cap + rank)[0:feats, :]
    first = place * per + lax.shift_right_logical(rank, 7)
    second = first + chunks
    low = rank & (LANES - 1)
    lengths = len_ref[...]
    one = jnp.where(lengths > 0, one_s[0:feats, :] + 1, 0)
    two = jnp.where(lengths > 1, two_s[0:feats, :] + 1, 0)
    at = iota((count, lanes), 0)
    lane_at = iota((LANES, lanes), 0)
    for f in range(feats):
        held = jnp.where(at == first[f : f + 1, :], one[f : f + 1, :], 0)
        held = jnp.where(at == second[f : f + 1, :], two[f : f + 1, :], held)
        span = slice(f * lanes, (f + 1) * lanes)
        a_s[0:count, span] = lax.shift_right_logical(held, 7).astype(F32).astype(BF16)
        a_s[count : 2 * count, span] = (held & 127).astype(F32).astype(BF16)
        b_s[:, span] = jnp.where(lane_at == low[f : f + 1, :], 1.0, 0.0).astype(BF16)
    found = dot(a_s[...], b_s[...], NT)
    req_ref[...] = (found[0:count] * 128.0 + found[count:]).astype(I32)


def update_kernel(
    local_ref, new_ref, versions_ref, table_ref, values_ref, rows_s, part_ref
):
    held_rows, width = table_ref.shape
    rows_s[0:held_rows, :] = table_ref[...]

    def entry(i, carry):
        at = local_ref[i]
        to = jnp.where(new_ref[i] > versions_ref[at], at, held_rows)
        rows_s[pl.ds(to, 1), :] = values_ref[pl.ds(i, 1), :]
        return carry

    lax.fori_loop(0, values_ref.shape[0], entry, 0, unroll=32)
    own_rows = part_ref.shape[0]
    start = pl.multiple_of(lax.axis_index("dp") * own_rows, own_rows)
    part_ref[...] = rows_s[pl.ds(start, own_rows), :].astype(BF16)


def lookup_kernel(peers, cap, partners, pieces, after_ref, ids_ref, table_ref, *refs):
    del after_ref
    mirror, outs, count_s = refs[:pieces], refs[pieces:-1], refs[-1]
    width = outs[0].shape[1]
    per = ids_ref.shape[0] // (2 * peers)
    chunks = -(-cap // LANES)
    one, zero = jnp.ones((), BF16), jnp.zeros((), BF16)
    at_dp = lax.axis_index("dp")
    at_table = lax.rem(lax.axis_index("table"), peers)
    own_rows = mirror[0].shape[0]
    bases = [lax.rem(at_dp + pieces - p, pieces) * own_rows for p in range(pieces)]
    spans = [[(0, table_ref.shape[0])], [(base, own_rows) for base in bases]]

    def count(kind):
        for g, partner in enumerate(partners):
            start = ((at_table ^ partner) * 2 + kind) * per
            block = ids_ref[pl.ds(pl.multiple_of(start, 8), per), :].T
            for c in range(chunks):
                n = min(LANES, cap - c * LANES)
                at = g * cap + c * LANES
                a = jnp.broadcast_to(block[0:n, c : c + 1], (n, LANES))
                b = jnp.broadcast_to(block[0:n, chunks + c : chunks + c + 1], (n, LANES))
                column = 0
                for base, rows in spans[kind]:
                    a16, b16 = (a - base).astype(I16), (b - base).astype(I16)
                    for k in range(0, rows, LANES):
                        size = min(LANES, rows - k)
                        row = (iota((n, size), 1) + (1 + k)).astype(I16)
                        count_s[kind, at : at + n, column : column + size] = jnp.where(
                            a16[:, :size] == row, one, zero
                        ) + jnp.where(b16[:, :size] == row, one, zero)
                        column += size

    def give(kind, found):
        for g, out in enumerate(outs):
            out[kind * cap : (kind + 1) * cap, :] = found[g * cap : (g + 1) * cap, :].astype(BF16)

    count(0)
    count(1)
    both = dot(count_s[0], table_ref[...])
    give(0, both[:, 0:width] + both[:, width:])
    found = dot(count_s[1, :, 0:own_rows], mirror[0][...])
    for p in range(1, pieces):
        found = found + dot(count_s[1, :, p * own_rows : (p + 1) * own_rows], mirror[p][...])
    give(1, found)


def dense_kernel(pieces, partners, cap, *refs):
    answers, refs = refs[:partners], refs[partners:]
    pos_ref, dense_ref, labels_ref = refs[0:3]
    bias_ref, head_ref, logit_ref = refs[3 + 2 * pieces : 6 + 2 * pieces]
    native_ref, mirror_ref, rows_s, x_s, factor_s, bags_s, down_s, up_s, sems = refs[
        6 + 2 * pieces :
    ]
    at_table = lax.rem(lax.axis_index("table"), partners)
    load_down = pltpu.make_async_copy(refs[3], down_s, sems.at[0])
    load_up = pltpu.make_async_copy(refs[3 + pieces], up_s, sems.at[1])
    load_down.start()
    load_up.start()
    down = (down_s,) + refs[4 : 3 + pieces]
    up = (up_s,) + refs[4 + pieces : 3 + 2 * pieces]
    feats, samples = pos_ref.shape
    width = dense_ref.shape[1]
    for p, answer in enumerate(answers):
        for kind in range(2):
            at = pl.multiple_of((kind * partners + (at_table ^ p)) * cap, 16)
            rows_s[pl.ds(at, cap), :] = answer[kind * cap : (kind + 1) * cap, :].astype(F32)

    def fetch(f, carry):
        start = f * samples
        for b in range(samples):
            bags_s[pl.ds(start + b, 1), :] = rows_s[pl.ds(pos_ref[f, b], 1), :]
        return carry

    lax.fori_loop(0, feats, fetch, 0)
    x_s[:, 0:width] = dense_ref[...]
    for f in range(feats):
        x_s[:, (f + 1) * width : (f + 2) * width] = bags_s[
            f * samples : (f + 1) * samples, :
        ].astype(BF16)
    load_down.wait()
    x = x_s[...]
    crossed = [dot(x, w[...]).astype(BF16) for w in down]
    load_up.wait()
    total = jnp.zeros((samples, width), F32)
    wide = x_s.shape[1]
    step = 2 * width
    spans = [slice(k, min(k + step, wide)) for k in range(0, wide, step)]
    for span in spans:
        factor = bias_ref[:, span]
        for c, w in zip(crossed, up):
            factor = factor + dot(c, w[:, span])
        factor_s[:, span] = factor
        base = x_s[:, span].astype(F32)
        terms = (base * factor + base) * head_ref[:, span]
        for k in range(0, terms.shape[1], width):
            total = total + terms[:, k : k + width]
    logits = jnp.sum(total, axis=1, keepdims=True)
    logit_ref[...] = jnp.broadcast_to(logits, (samples, samples)).T[0:1, :]
    labels = jnp.broadcast_to(labels_ref[...].astype(F32), (samples, samples)).T[:, 0:1]
    signal = loss_scale * (jax.nn.sigmoid(logits) - labels)
    lifts = []
    for span in spans:
        lifts.append(((signal * head_ref[:, span]) * x_s[:, span].astype(F32)).astype(BF16))
    lift = jnp.concatenate(lifts, axis=1)
    back = [dot(w[...], lift, NT).astype(BF16) for w in up]
    for start in range(width, wide, step):
        span = slice(start, min(start + step, wide))
        outer = signal * head_ref[:, span]
        turned = 0.0
        for c, w in zip(back, down):
            turned = turned + dot(w[span, :], c)
        grad = outer + turned.T + outer * factor_s[:, span]
        for k in range(0, grad.shape[1], width):
            f = (start + k) // width - 1
            bags_s[f * samples : (f + 1) * samples, :] = grad[:, k : k + width]

    def place(f, carry):
        start = f * samples
        for b in range(samples):
            rows_s[pl.ds(pos_ref[f, b], 1), :] = bags_s[pl.ds(start + b, 1), :]
        return carry

    lax.fori_loop(0, feats, place, 0)
    native_ref[...] = rows_s[0 : partners * cap, :].astype(BF16)
    mirror_ref[...] = rows_s[partners * cap :, :].astype(BF16)


def scatter_kernel(by, replicas, after_ref, *refs):
    del after_ref
    ids, grads, (out_ref, bags_s) = refs[:replicas], refs[replicas:-2], refs[-2:]
    rows = out_ref.shape[0]
    tile = min(rows, 512)
    each = ids[0].shape[0] // 2
    slots = each * LANES
    step = 4 if each % 4 == 0 else 1
    one, zero = jnp.ones((), BF16), jnp.zeros((), BF16)
    at = (iota((tile, LANES), 0) + 1).astype(I16)
    start = 0
    for grad in grads:
        bags_s[start : start + grad.shape[0], :] = grad[...]
        start += grad.shape[0]
    first = lax.rem(lax.axis_index("dp") + by, lax.axis_size("dp")) * rows
    for start in range(0, rows, tile):
        base = first + start
        total = jnp.zeros((tile, LANES), F32)
        for r, lines in enumerate(ids):
            for k in range(0, each, step):
                counts = []
                for line in range(k, k + step):
                    a = lines[line : line + 1, :] - base
                    b = lines[each + line : each + line + 1, :] - base
                    a = jnp.broadcast_to(a, (tile, LANES)).astype(I16)
                    b = jnp.broadcast_to(b, (tile, LANES)).astype(I16)
                    counts.append(jnp.where(a == at, one, zero) + jnp.where(b == at, one, zero))
                here = r * slots + k * LANES
                total = total + dot(
                    jnp.concatenate(counts, axis=1), bags_s[here : here + step * LANES, :]
                )
        out_ref[start : start + tile, :] = total


def call(kernel, outs, ins, scratch=(), flops=1024, moved=1024):
    cost = pl.CostEstimate(flops=flops, bytes_accessed=moved, transcendentals=0)
    return pl.pallas_call(
        kernel,
        out_shape=outs,
        in_specs=ins,
        out_specs=jax.tree.map(lambda _: VMEM, outs),
        scratch_shapes=list(scratch),
        compiler_params=params,
        cost_estimate=cost,
    )


def in_hbm(x):
    return pltpu.with_memory_space_constraint(x, pltpu.HBM)


def in_vmem(x):
    return pltpu.with_memory_space_constraint(x, pltpu.VMEM)


def shape(dims, dtype):
    return jax.ShapeDtypeStruct(dims, dtype)


def body(
    emb_table,
    versions,
    conf_local,
    conf_version,
    conf_values,
    owners,
    row_local,
    lengths,
    dense_out,
    labels,
    cross_down,
    cross_up,
    cross_bias,
    head_weight,
):
    peers, replicas = lax.axis_size("table"), lax.axis_size("dp")
    half = peers // 2
    groups = [list(range(half)), list(range(half, peers))]
    rows_dev, width = emb_table.shape
    samples, feats, slots = row_local.shape
    cap = round_up(3 * samples * feats // (2 * peers), 16)
    chunks = -(-cap // LANES)
    per = round_up(slots * chunks, 8)
    lines_half = half * cap // LANES
    wide = cross_down.shape[1]
    own_rows = rows_dev // replicas

    def shift(x, by):
        if by == 0:
            return x
        return lax.ppermute(x, "dp", [(i, (i + by) % replicas) for i in range(replicas)])

    def across(x):
        far = half + half // 2
        return lax.ppermute(x, "table", [(i, i ^ far) for i in range(peers)])

    def exchange(x):
        return lax.all_to_all(
            x, "table", split_axis=0, concat_axis=0, axis_index_groups=groups, tiled=True
        )


    rows, part = call(
        update_kernel,
        (shape((rows_dev + 8, width), F32), shape((own_rows, width), BF16)),
        [SMEM] * 3 + [VMEM] * 2,
    )(*map(in_hbm, (conf_local, conf_version, versions, emb_table, conf_values)))
    position, requests, table = call(
        functools.partial(route_kernel, peers, cap),
        (
            shape((feats, samples), I32),
            shape((peers * per, LANES), I32),
            shape((rows_dev, 2 * width), BF16),
        ),
        [VMEM] * 4,
        [pltpu.VMEM((round_up(feats, 8), samples), I32)] * 3
        + [
            pltpu.VMEM((2 * peers * per, feats * samples), BF16),
            pltpu.VMEM((LANES, feats * samples), BF16),
        ],
    )(rows, *map(in_hbm, (owners.transpose(1, 2, 0), row_local.transpose(1, 2, 0), lengths.T)))
    down = [shift(cross_down[0], by) for by in range(replicas)]
    up = [shift(cross_up[0], by) for by in range(replicas)]
    asked = exchange(requests.reshape(half, 2 * per, LANES)).reshape(2 * half * per, LANES)
    part = across(part)
    part, asked = lax.optimization_barrier((part, asked))
    mirror = [shift(part, by) for by in range(replicas)]
    asked, down, up = lax.optimization_barrier((asked, down, up))

    def meet(x, partner):
        if partner == 0:
            return x
        return lax.ppermute(x, "table", [(i, i ^ partner) for i in range(peers)])

    steps = 4 if half % 8 == 0 else 1
    pairs = [(i, half - 1 - i) for i in range(half // 2, half)]
    group = len(pairs) // steps
    answers = [None] * half
    after = [asked, asked, asked]
    for start in range(len(pairs) - group, -1, -group):
        partners = [p for pair in pairs[start : start + group] for p in pair]
        found = call(
            functools.partial(lookup_kernel, half, cap, partners, replicas),
            tuple(shape((2 * cap, width), BF16) for _ in partners),
            [ANY] + [VMEM] * (2 + replicas),
            [pltpu.VMEM((2, 2 * group * cap, rows_dev), BF16)],
        )(after[-3], asked, table, *mirror)
        for partner, sums in zip(partners, found):
            answers[partner] = meet(sums, partner)
        after.append(answers[partners[0]])

    logits, to_native, to_mirror = call(
        functools.partial(dense_kernel, replicas, half, cap),
        (shape((1, samples), F32),) + (shape((half * cap, width), BF16),) * 2,
        [VMEM] * half + [SMEM] + [VMEM] * 2 + ([ANY] + [VMEM] * (replicas - 1)) * 2 + [VMEM] * 2,
        [
            pltpu.VMEM((peers * cap, width), F32),
            pltpu.VMEM((samples, wide), BF16),
            pltpu.VMEM((samples, wide), F32),
            pltpu.VMEM((samples * feats, width), F32),
            pltpu.VMEM(down[0].shape, BF16),
            pltpu.VMEM(up[0].shape, BF16),
            pltpu.SemaphoreType.DMA((2,)),
        ],
    )(
        *map(in_vmem, answers),
        position,
        dense_out,
        labels.reshape(1, samples),
        in_hbm(down[0]),
        *map(in_vmem, down[1:]),
        in_hbm(up[0]),
        *map(in_vmem, up[1:]),
        cross_bias,
        head_weight.reshape(1, wide),
    )
    ids = asked.reshape(half, 2, per, LANES)
    got_mirror = exchange(to_mirror.reshape(half, cap, width)).reshape(half * cap, width)
    got_mirror = in_vmem(got_mirror)

    def lines_of(kind):
        return jnp.concatenate(
            [
                ids[:, kind, slot * chunks : (slot + 1) * chunks]
                .reshape(half, chunks * LANES)[:, :cap]
                .reshape(lines_half, LANES)
                for slot in range(slots)
            ]
        )

    def scatter(by, after, lines, grads):
        return call(
            functools.partial(scatter_kernel, by, len(lines)),
            shape((own_rows, width), F32),
            [ANY] + [VMEM] * (len(lines) + len(grads)),
            [pltpu.VMEM((len(lines) * half * cap, width), BF16)],
        )(after, *lines, *grads)

    mirror_lines, native_lines = lines_of(1), lines_of(0)
    last, parts = asked, []
    for by in range(1, replicas):
        last = scatter(by, last, [mirror_lines], [got_mirror])
        parts.append(shift(last, by))
    last, to_native = lax.optimization_barrier((last, to_native))
    whole_native = exchange(to_native.reshape(half, cap, width)).reshape(half * cap, width)
    got_native = in_vmem(whole_native)
    own = scatter(0, last, [mirror_lines], [got_mirror])
    mirrored = functools.reduce(jnp.add, [own] + parts).astype(BF16)
    returned = across(mirrored)
    _, native_lines = lax.optimization_barrier((mirrored, native_lines))
    every_line = [shift(native_lines, by) for by in range(replicas)]
    pieces = 4 if half * cap % 64 == 0 else 1
    size = half * cap // pieces
    every_got = [got_native]
    for by in range(1, replicas):
        for i in range(pieces):
            every_got.append(in_vmem(shift(whole_native[i * size : (i + 1) * size], by)))
    grads = scatter(0, mirrored, every_line, every_got) + returned.astype(F32)
    return (logits.reshape(samples), grads)


def solution(mesh):
    in_specs = (
        P("table", None),
        P("table"),
        P("table"),
        P("table"),
        P("table", None),
        P(("table", "dp"), None, None),
        P(("table", "dp"), None, None),
        P(("table", "dp"), None),
        P(("table", "dp"), None),
        P(("table", "dp")),
        P(None, None, "dp"),
        P(None, "dp", None),
        P(),
        P(),
    )
    out_specs = (P(("table", "dp")), P(("table", "dp"), None))
    return jax.shard_map(body, mesh=mesh, in_specs=in_specs, out_specs=out_specs, check_vma=False)
```
